256 devices in a mesh: seq: 64 (over x_lo, z, y), tp: 4 (over x_hi, core).
Axes of the slice: x: 4 (x_hi: 2, x_lo: 2; x = x_hi * 2 + x_lo), y: 4, z: 8, core: 2. Of those that a mesh axis runs over, the one named last changes fastest.
Arguments:
- queries: bfloat16 [8192, 8192], P('seq', 'tp'), may hold values from -150 to 150
- comp_keys: bfloat16 [8192, 1024], P('seq', 'tp'), may hold values from -9 to 9
- comp_values: bfloat16 [8192, 1024], P('seq', 'tp'), may hold values from -6 to 6
- prompt_keys: bfloat16 [8192, 1024], P('seq', 'tp'), may hold values from -6 to 6
- prompt_values: bfloat16 [8192, 1024], P('seq', 'tp'), may hold values from -6 to 6
- page_table: int32 [64], P('seq'), may hold values from 0 to 63, each once
- lengths: int32 [64], P('seq'), may hold values from 1 to 128, 5120 in all
- out_weight: bfloat16 [64, 128, 4096], P('tp', 'seq'), may hold values from -0.0625 to 0.0625
Outputs:
- projected: bfloat16 [8192, 4096], P('seq', 'tp')
The draws below stay inside these ranges and needn't reach their ends.
All inputs are finite; a program needn't handle non-finite values. No bound on the sum of `lengths` on one device may be relied on, other than what follows from the above.
Results may differ from the reference program's by a relative error of at most 0.018.
Values may be sent and summed in bfloat16 or wider, within the bound.
No kernel may reach another device: no remote copies, remote signals or barrier semaphores. Data moves between devices by JAX's collectives and lax.ppermute only.
A program may use at most 128 MiB of HBM per device.

```python
import math
import jax
import jax.numpy as jnp
import numpy as np
from jax import lax

HQ = 64
KVH = 8
HD = 128
DOUT = 4096
WIN = 128
PAGE = 128
COMPLETIONS = 64
ROWS = 8192
PROMPT = 8192
N_SEQ = 64


def shared_keys(key):
    return jnp.clip(jax.random.normal(key, (ROWS, KVH * HD), jnp.float32), -6.0, 6.0)


def draw_comp_keys(key, part):
    base = shared_keys(key)
    return base.astype(jnp.bfloat16)


def draw_queries(key, part):
    key = jax.random.fold_in(key, 7)
    values = jnp.clip(jax.random.normal(key, (ROWS, HQ, HD), jnp.float32), -6.0, 6.0)
    return values.reshape(ROWS, HQ * HD).astype(jnp.bfloat16)


def block_levels(rng, dims, split, least, top_value):
    gain, own = 1.0, jax.random.fold_in(rng, 6)
    for position, blocks in split:
        steps = jnp.exp(jax.random.uniform(jax.random.fold_in(own, position), (blocks,), jnp.float32, least / len(split), top_value / len(split)))
        gain = gain * jnp.repeat(steps, dims[position] // blocks).reshape([-1 if axis == position else 1 for axis in range(len(dims))])
    return gain


def profile(number_of, total, reach, skew):
    portions = [(1 << 20) // math.isqrt(grade ** skew) + 1 for grade in range(2, number_of + 1)]
    rest, given = total - reach - (number_of - 1), [1] * (number_of - 1)
    while rest > 0:
        candidates = [i for i in range(number_of - 1) if given[i] < reach]
        whole, budget = sum([portions[i] for i in candidates]), rest
        for i in candidates:
            addition = min(reach - given[i], max(1, budget * portions[i] // whole), rest)
            given[i] = given[i] + addition
            rest = rest - addition
    return np.array([reach] + given)


def uneven(own_key, number_of, total, bound, skew):
    if number_of == 2:
        one = jax.random.randint(own_key, (), max(1, total - bound), min(bound, total - 1) + 1)
        return jnp.stack([one, total - one])
    tallies = jnp.asarray(profile(number_of, total, bound, skew), jnp.int32)
    couples = (number_of - 1) // 2
    source_of, sink = tallies[1:1 + 2 * couples:2], tallies[2:2 + 2 * couples:2]
    slack = jnp.minimum(source_of - 1, bound - sink)
    shifted = jax.random.randint(jax.random.fold_in(own_key, 1), (couples,), 0, 1 << 20) % (slack + 1)
    tallies = tallies.at[1:1 + 2 * couples:2].set(source_of - shifted).at[2:2 + 2 * couples:2].set(sink + shifted)
    return tallies[jax.random.permutation(jax.random.fold_in(own_key, 2), number_of)]


def scatter_about(rng, extent, deviation, reach, split=(), held_as=jnp.bfloat16):
    factor_of = block_levels(rng, extent, split, -0.22, 0.18) if split else 1.0
    entries = jax.random.normal(rng, extent, jnp.float32) * deviation * factor_of
    return jnp.minimum(jnp.maximum(entries, -reach), reach).astype(held_as)


def setup_inputs(seed: int = 0) -> dict:
    key_list = jax.random.split(jax.random.key(seed), 9)
    return {
        "queries": draw_queries(jax.random.fold_in(key_list[8], 71), 0),
        "comp_keys": draw_comp_keys(jax.random.fold_in(key_list[8], 71), 0),
        "comp_values": scatter_about(key_list[2], (ROWS, KVH * HD), 1.0, 6.0, ((0, 64), (1, 4))),
        "prompt_keys": scatter_about(key_list[3], (PROMPT, KVH * HD), 1.0, 6.0, ((0, 64), (1, 4))),
        "prompt_values": scatter_about(key_list[4], (PROMPT, KVH * HD), 1.0, 6.0, ((0, 64), (1, 4))),
        "page_table": jax.random.permutation(key_list[5], N_SEQ).astype(jnp.int32),
        "lengths": uneven(key_list[6], COMPLETIONS, COMPLETIONS * WIN * 5 // 8, WIN, 0).astype(jnp.int32),
        "out_weight": scatter_about(key_list[7], (HQ, HD, DOUT), (HQ * HD) ** -0.5, 0.0625, ((0, 4), (1, 64))),
    }


theta_base = 1000000.0


def rotate(block, positions):
    half = block.shape[-1] // 2
    freq = jnp.power(jnp.float32(theta_base), -2.0 * jnp.arange(half, dtype=jnp.float32) / block.shape[-1])
    angle = positions.astype(jnp.float32)[:, None] * freq[None, :]
    cosine = jnp.cos(angle)[:, None, :]
    sine = jnp.sin(angle)[:, None, :]
    first = block[..., :half]
    second = block[..., half:]
    return jnp.concatenate([first * cosine - second * sine, second * cosine + first * sine], axis=-1)


def reference(queries, comp_keys, comp_values, prompt_keys, prompt_values, page_table, lengths, out_weight):
    group = HQ // KVH
    rows_all = jnp.arange(PROMPT, dtype=jnp.int32)
    ppos = page_table[rows_all // PAGE] * PAGE + rows_all % PAGE
    pkeys = rotate(prompt_keys.astype(jnp.float32).reshape(PROMPT, KVH, HD), ppos).astype(jnp.bfloat16)
    pvals = prompt_values.reshape(PROMPT, KVH, HD)
    slots = jnp.arange(WIN, dtype=jnp.int32)
    qpos = PROMPT + slots
    weight_flat = out_weight.reshape(HQ * HD, DOUT)
    scale = 1.0 / (HD ** 0.5)

    def one(items):
        qblk, kblk, vblk, length = items
        qrot = rotate(qblk.astype(jnp.float32).reshape(WIN, HQ, HD), qpos).astype(jnp.bfloat16)
        qrot = qrot.reshape(WIN, KVH, group, HD)
        ckeys = rotate(kblk.astype(jnp.float32).reshape(WIN, KVH, HD), qpos).astype(jnp.bfloat16)
        cvals = vblk.reshape(WIN, KVH, HD)
        keys = jnp.concatenate([pkeys, ckeys], axis=0).astype(jnp.float32)
        vals = jnp.concatenate([pvals, cvals], axis=0).astype(jnp.float32)
        scores = jnp.einsum("rkgd,jkd->kgrj", qrot.astype(jnp.float32), keys) * scale
        own = (slots[None, :] <= slots[:, None]) & (slots[None, :] < length)
        mask = jnp.concatenate([jnp.ones((WIN, PROMPT), bool), own], axis=1)
        scores = jnp.where(mask[None, None], scores, -jnp.inf)
        top = jnp.max(scores, axis=-1, keepdims=True)
        weights = jnp.exp(scores - top)
        total = jnp.sum(weights, axis=-1)
        summed = jnp.einsum("kgrj,jkd->kgrd", weights.astype(jnp.bfloat16).astype(jnp.float32), vals)
        attended = summed / total[..., None]
        attended = jnp.where((slots < length)[None, None, :, None], attended, 0.0)
        attended = attended.transpose(2, 0, 1, 3).reshape(WIN, HQ * HD).astype(jnp.bfloat16)
        return jnp.dot(attended, weight_flat, preferred_element_type=jnp.float32).astype(jnp.bfloat16)

    result = lax.map(one, (queries.reshape(COMPLETIONS, WIN, HQ * HD), comp_keys.reshape(COMPLETIONS, WIN, KVH * HD), comp_values.reshape(COMPLETIONS, WIN, KVH * HD), lengths))
    return result.reshape(ROWS, DOUT)
```

```python
import functools
import math

import jax
import jax.numpy as jnp
from jax import lax
from jax.experimental import pallas as pl
from jax.experimental.pallas import tpu as pltpu
from jax.sharding import PartitionSpec as P

theta_base = 1000000.0
XL, NZ, NY = 2, 8, 4
LOG2E = math.log2(math.e)
VMEM = 56 * 2**20


def seq_id(x, z, y):
    return ((x % XL) * NZ + z % NZ) * NY + y % NY


def seq_perm(dx, dz, dy):
    return [
        (seq_id(x, z, y), seq_id(x + dx, z + dz, y + dy))
        for x in range(XL)
        for z in range(NZ)
        for y in range(NY)
    ]


def both_perm(dx, dt):
    return [
        (4 * seq_id(x, z, y) + t, 4 * seq_id(x + dx, z, y) + t ^ dt)
        for x in range(XL)
        for z in range(NZ)
        for y in range(NY)
        for t in range(4)
    ]


def along_z(x, k):
    return lax.ppermute(x, "seq", seq_perm(0, k, 0))


def along_y(x, k):
    return lax.ppermute(x, "seq", seq_perm(0, 0, k))


def across(x):
    return lax.ppermute(x, "seq", seq_perm(1, 0, 0))


def gather_pages(page):
    block = jnp.concatenate([page] + [along_y(page, k) for k in range(1, NY)], axis=0)
    up = down = block
    blocks = [block]
    for _ in range(1, NZ // 2):
        up, down = along_z(up, 1), along_z(down, -1)
        blocks += [up, down]
    half = block.shape[0] // 2
    blocks += [along_z(up[:half], 1), along_z(down[half:], -1)]
    return blocks


def tables(positions, size):
    half = size // 2
    freq = jnp.power(
        jnp.float32(theta_base), -2.0 * jnp.arange(half, dtype=jnp.float32) / size
    )
    angle = positions.astype(jnp.float32)[:, None] * freq[None, :]
    cosine, sine = jnp.cos(angle), jnp.sin(angle)
    return jnp.concatenate([cosine, cosine], -1), jnp.concatenate([-sine, sine], -1)


def prepare_kernel(qc, qs, kc, ks, q, ckey, pkey, pval, q_out, c_out, kv0_out, kv1_out):
    def turn(block, cosine, sine):
        block = block.astype(jnp.float32)
        return (block * cosine + pltpu.roll(block, 64, 1) * sine).astype(jnp.bfloat16)

    for h in range(q.shape[1] // 128):
        cols = slice(h * 128, h * 128 + 128)
        q_out[:, cols] = turn(q[:, cols], qc[...], qs[...])
    for k, out in enumerate((kv0_out, kv1_out)):
        cols = slice(k * 128, k * 128 + 128)
        c_out[:, cols] = turn(ckey[:, cols], qc[...], qs[...])
        out[:, :128] = turn(pkey[:, cols], kc[...], ks[...])
        out[:, 128:] = pval[:, cols]


def prepare(qc, qs, kc, ks, q, ckey, pkey, pval):
    win = q.shape[0]
    kv = jax.ShapeDtypeStruct((win, 256), jnp.bfloat16)
    return pl.pallas_call(
        prepare_kernel,
        out_shape=[
            jax.ShapeDtypeStruct(q.shape, jnp.bfloat16),
            jax.ShapeDtypeStruct(ckey.shape, jnp.bfloat16),
            kv,
            kv,
        ],
        compiler_params=pltpu.CompilerParams(vmem_limit_bytes=VMEM),
    )(qc, qs, kc, ks, q, ckey, pkey, pval)


def attend_kernel(length, q_own, q_peer, ckey, cval, *refs, heads, scale):
    *blocks, out, stats = refs
    step = pl.program_id(0)
    win = q_own.shape[0]
    rows = 2 * win
    lane = lax.broadcasted_iota(jnp.int32, (rows, 128), 1)
    row = lax.broadcasted_iota(jnp.int32, (rows, win), 0)
    slot = lax.broadcasted_iota(jnp.int32, (rows, win), 1)
    own = (slot <= row) & (slot < length[0]) & (row < win)
    found = jnp.zeros((rows, 128), jnp.float32)
    for h in range(heads):
        cols = slice(h * 128, h * 128 + 128)
        q = jnp.concatenate([q_own[:, cols], q_peer[:, cols]], axis=0)
        top = acc = None
        for index in range(len(blocks) + 1):
            if index < len(blocks):
                keys, values = blocks[index][:, :128], blocks[index][:, 128:]
            else:
                keys, values = ckey[...], cval[...]
            scores = lax.dot_general(
                q, keys, (((1,), (1,)), ((), ())), preferred_element_type=jnp.float32
            )
            if index == len(blocks):
                scores = jnp.where(own, scores, -jnp.inf)
            wide = jnp.concatenate([values, jnp.ones_like(values)], axis=1)
            new_top = jnp.max(scores, axis=-1, keepdims=True)
            if top is not None:
                new_top = jnp.maximum(top, new_top)
            weights = jnp.exp2((scores - new_top) * scale).astype(jnp.bfloat16)
            part = jnp.dot(weights, wide, preferred_element_type=jnp.float32)
            if acc is None:
                acc = part
            else:
                acc = acc * jnp.exp2((top - new_top) * scale) + part
            top = new_top
        total = acc[:, 128:]
        out[:, cols] = (acc[:, :128] / total).astype(jnp.bfloat16)
        number = step * heads + h
        found = jnp.where(lane == number, top * scale, found)
        found = jnp.where(lane == number + 64, total, found)
    mine = (lane % 64) // heads == step

    @pl.when(step == 0)
    def _():
        stats[...] = found

    @pl.when(step > 0)
    def _():
        stats[...] = jnp.where(mine, found, stats[...])


def attend(length, q_own, q_peer, ckey, cval, blocks, kv_head, group, scale):
    heads = 2
    win = q_own.shape[0]
    steps = group // heads
    keys = sum(b.shape[0] for b in blocks) + win
    one = pl.BlockSpec((win, 128), lambda s: (0, kv_head))
    qspec = pl.BlockSpec((win, 128 * heads), lambda s: (0, kv_head * steps + s))
    return pl.pallas_call(
        functools.partial(attend_kernel, heads=heads, scale=scale),
        grid=(steps,),
        in_specs=[pl.BlockSpec(memory_space=pltpu.SMEM), qspec, qspec, one, one]
        + [pl.BlockSpec(b.shape, lambda s: (0, 0)) for b in blocks],
        out_specs=[
            pl.BlockSpec((2 * win, 128 * heads), lambda s: (0, s)),
            pl.BlockSpec((2 * win, 128), lambda s: (0, 0)),
        ],
        out_shape=[
            jax.ShapeDtypeStruct((2 * win, 128 * group), jnp.bfloat16),
            jax.ShapeDtypeStruct((2 * win, 128), jnp.float32),
        ],
        compiler_params=pltpu.CompilerParams(vmem_limit_bytes=VMEM),
        cost_estimate=pl.CostEstimate(
            flops=2 * win * group * keys * 128 * 8,
            bytes_accessed=4 * 2**20,
            transcendentals=2 * win * group * keys,
        ),
    )(length, q_own, q_peer, ckey, cval, *blocks)


def merge_kernel(plane, *refs, group):
    *ins, out = refs
    kv_heads = len(ins) // 4
    rows = out.shape[0]
    win = rows // 2
    features = out.shape[1]
    row = lax.broadcasted_iota(jnp.int32, (256, 1), 0)
    column = lax.broadcasted_iota(jnp.int32, (256, features), 1)

    def swap(block):
        return jnp.concatenate([block[win:], block[:win]], axis=0)

    total = None
    for k in range(kv_heads):
        mine, mine_stats, peer, peer_stats = ins[4 * k : 4 * k + 4]
        a, b = mine_stats[...], swap(peer_stats[...])
        top = jnp.maximum(a, b)
        for pair in range(group // 2):
            joined = []
            for g in (2 * pair, 2 * pair + 1):
                cols = slice(g * 128, g * 128 + 128)
                one = a[:, g + 64 : g + 65] * jnp.exp2(a[:, g : g + 1] - top[:, g : g + 1])
                two = b[:, g + 64 : g + 65] * jnp.exp2(b[:, g : g + 1] - top[:, g : g + 1])
                inverse = 1.0 / (one + two)
                joined.append(
                    (
                        mine[:, cols].astype(jnp.float32) * (one * inverse)
                        + swap(peer[:, cols]).astype(jnp.float32) * (two * inverse)
                    ).astype(jnp.bfloat16)
                )
            attended = jnp.concatenate(joined, axis=1)
            head = k * group + 2 * pair + row // 128
            feature = row % 128
            other = (feature // 64) ^ plane[0]
            target = (feature % 64) // 2 * 64 + other * 32 + head * 2 + feature % 2
            order = jnp.where(column == target, 1.0, 0.0).astype(jnp.bfloat16)
            part = jnp.dot(attended, order, preferred_element_type=jnp.float32)
            total = part if total is None else total + part
    out[...] = total.astype(jnp.bfloat16)


def merge(plane, parts, group):
    rows = parts[0].shape[0]
    features = 128 * group * (len(parts) // 4)
    return pl.pallas_call(
        functools.partial(merge_kernel, group=group),
        in_specs=[pl.BlockSpec(memory_space=pltpu.SMEM)]
        + [pl.BlockSpec(memory_space=pltpu.VMEM)] * len(parts),
        out_shape=jax.ShapeDtypeStruct((rows, features), jnp.bfloat16),
        compiler_params=pltpu.CompilerParams(vmem_limit_bytes=VMEM),
        cost_estimate=pl.CostEstimate(
            flops=2 * rows * features * features,
            bytes_accessed=3 * 2**20,
            transcendentals=0,
        ),
    )(plane, *parts)


def per_device(
    queries, comp_keys, comp_values, prompt_keys, prompt_values, page_table, lengths, out_weight
):
    win = queries.shape[0]
    head_size = 128
    heads = queries.shape[1] // head_size
    kv_heads = comp_keys.shape[1] // head_size
    group = heads // kv_heads
    page = prompt_keys.shape[0]
    seq_count = XL * NZ * NY
    features = out_weight.shape[2]
    block = features // 8
    seq_index = lax.axis_index("seq")
    tp_index = lax.axis_index("tp")
    plane = seq_index // (NZ * NY)
    slots = jnp.arange(win, dtype=jnp.int32)

    halves = out_weight.reshape(heads * 2, 4, 2, block)
    keep = jnp.where(plane == 0, halves[:, :, 0], halves[:, :, 1]).reshape(heads * 2, 4 * block)
    give = jnp.where(plane == 0, halves[:, :, 1], halves[:, :, 0]).reshape(heads * 2, 4 * block)
    rows = jnp.concatenate([keep, across(give)], axis=0)
    groups = [[seq_id(x, 0, 0) + i for i in range(NZ * NY)] for x in range(XL)]
    weight = lax.all_gather(rows, "seq", axis=0, tiled=True, axis_index_groups=groups)

    qc, qs = tables(page * seq_count + slots, head_size)
    kc, ks = tables(page_table[0] * page + jnp.arange(page, dtype=jnp.int32), head_size)
    qrot, ckeys, *pages = prepare(
        qc, qs, kc, ks, queries, comp_keys, prompt_keys, prompt_values
    )
    q_peer = across(qrot)
    parts = []
    scale = LOG2E / math.sqrt(head_size)
    gathered = [gather_pages(p) for p in pages]
    for k in range(kv_heads):
        out, stats = attend(
            lengths, qrot, q_peer, ckeys, comp_values, gathered[k], k, group, scale
        )
        parts += [out, stats, across(out), across(stats)]
    attended = merge(plane.reshape(1), parts, group)
    partial_value = jnp.dot(attended, weight, preferred_element_type=jnp.float32)
    partial_value = partial_value.astype(jnp.bfloat16).reshape(2 * win, 2, 2, block)

    core, far = tp_index % 2, tp_index // 2
    give = jnp.where(core == 0, partial_value[:, :, 1], partial_value[:, :, 0])
    keep = jnp.where(core == 0, partial_value[:, :, 0], partial_value[:, :, 1])
    came = lax.ppermute(give, "tp", [(0, 1), (1, 0), (2, 3), (3, 2)])
    chip = (keep.astype(jnp.float32) + came.astype(jnp.float32)).astype(jnp.bfloat16)
    near_block = jnp.where(far == 0, chip[:, 0], chip[:, 1])
    far_block = jnp.where(far == 0, chip[:, 1], chip[:, 0])
    axes = ("seq", "tp")
    one = lax.ppermute(far_block[:win], axes, both_perm(0, 2))
    two = lax.ppermute(near_block[win:], axes, both_perm(1, 0))
    three = lax.ppermute(far_block[win:], axes, both_perm(1, 2))
    mine = near_block[:win].astype(jnp.float32) + one.astype(jnp.float32)
    theirs = two.astype(jnp.float32) + three.astype(jnp.float32)
    first = jnp.where(plane == 0, mine, theirs)
    second = jnp.where(plane == 0, theirs, mine)
    result = jnp.concatenate([first, second], axis=1)
    return jnp.where((slots < lengths[0])[:, None], result, 0.0).astype(jnp.bfloat16)


def solution(mesh):
    in_specs = (
        P("seq", "tp"),
        P("seq", "tp"),
        P("seq", "tp"),
        P("seq", "tp"),
        P("seq", "tp"),
        P("seq"),
        P("seq"),
        P("tp", "seq", None),
    )
    out_specs = P("seq", "tp")
    return jax.shard_map(
        per_device, mesh=mesh, in_specs=in_specs, out_specs=out_specs, check_vma=False
    )
```

```python
import functools
import math

import jax
import jax.numpy as jnp
from jax import lax
from jax.experimental import pallas as pl
from jax.experimental.pallas import tpu as pltpu
from jax.sharding import PartitionSpec as P

theta_base = 1000000.0
XL, NZ, NY = 2, 8, 4
LOG2E = math.log2(math.e)
VMEM = 56 * 2**20
HEADS = 4


def seq_id(x, z, y):
    return ((x % XL) * NZ + z % NZ) * NY + y % NY


def seq_perm(dx, dz, dy):
    return [
        (seq_id(x, z, y), seq_id(x + dx, z + dz, y + dy))
        for x in range(XL)
        for z in range(NZ)
        for y in range(NY)
    ]


def both_perm(dx, dt):
    return [
        (4 * seq_id(x, z, y) + t, 4 * seq_id(x + dx, z, y) + t ^ dt)
        for x in range(XL)
        for z in range(NZ)
        for y in range(NY)
        for t in range(4)
    ]


def along_z(x, k):
    return lax.ppermute(x, "seq", seq_perm(0, k, 0))


def along_y(x, k):
    return lax.ppermute(x, "seq", seq_perm(0, 0, k))


def across(x):
    return lax.ppermute(x, "seq", seq_perm(1, 0, 0))


def tables(positions, size):
    half = size // 2
    freq = jnp.power(
        jnp.float32(theta_base), -2.0 * jnp.arange(half, dtype=jnp.float32) / size
    )
    angle = positions.astype(jnp.float32)[:, None] * freq[None, :]
    return jnp.cos(angle), jnp.sin(angle)


def prepare_kernel(
    plane, length, cosines, sines, q_own, q_give, ck_own, ck_give, cv_own, cv_give,
    pk_own, pk_give, pv_own, pv_give, q_out, pair_out, comp_out, kv_out, kv_give_out,
):
    win = q_own.shape[0]

    def table(rows):
        cosine, sine = cosines[rows, :], sines[rows, :]
        return (
            jnp.concatenate([cosine, cosine], axis=1),
            jnp.concatenate([-sine, sine], axis=1),
        )

    def turn(block, cosine, sine):
        block = block.astype(jnp.float32)
        return (block * cosine + pltpu.roll(block, 64, 1) * sine).astype(jnp.bfloat16)

    qc, qs = table(slice(0, win))
    kc, ks = table(slice(win, None))
    kv_give_out[:, :128] = turn(pk_give[...], kc, ks)
    kv_give_out[:, 128:] = pv_give[...]
    kv_out[:, :128] = turn(pk_own[...], kc, ks)
    kv_out[:, 128:] = pv_own[...]
    comp_out[:, :128] = turn(ck_own[...], qc, qs)
    comp_out[:, 128:] = cv_own[...]
    width = q_own.shape[1]
    for h in range(width // 128):
        cols = slice(h * 128, h * 128 + 128)
        q_out[:, cols] = turn(q_own[:, cols], qc, qs)
        pair_out[:, cols] = turn(q_give[:, cols], qc, qs)
    pair_out[:, width : width + 128] = turn(ck_give[...], qc, qs)
    pair_out[:, width + 128 : width + 256] = cv_give[...]
    pair_out[:, width + 256 :] = jnp.full(
        (win, 128), length[0].astype(jnp.float32), jnp.float32
    ).astype(jnp.bfloat16)


def prepare(plane, length, cosines, sines, q, ckey, cval, pkey, pval):
    win, width = q.shape[0], q.shape[1] // 2
    whole = pl.BlockSpec(cosines.shape, lambda s, p, n: (0, 0))
    specs, operands = [whole, whole], [cosines, sines]
    for array in (q, ckey, cval, pkey, pval):
        shape = (array.shape[0], array.shape[1] // 2)
        specs += [
            pl.BlockSpec(shape, lambda s, p, n: (0, p[0])),
            pl.BlockSpec(shape, lambda s, p, n: (0, 1 - p[0])),
        ]
        operands += [array, array]
    shapes = [(win, width), (win, width + 384), (win, 256), (win, 256), (win, 256)]
    return pl.pallas_call(
        prepare_kernel,
        grid_spec=pltpu.PrefetchScalarGridSpec(
            num_scalar_prefetch=2,
            grid=(1,),
            in_specs=specs,
            out_specs=[pl.BlockSpec(shape, lambda s, p, n: (0, 0)) for shape in shapes],
        ),
        out_shape=[jax.ShapeDtypeStruct(shape, jnp.bfloat16) for shape in shapes],
        compiler_params=pltpu.CompilerParams(vmem_limit_bytes=VMEM),
    )(plane, length, *operands)


def attend_kernel(length, q_own, q_peer, *refs, scale, heads, count, first, last):
    refs = list(refs)
    pairs = []
    for _ in range(count):
        block = refs.pop(0)
        pairs.append((block[:, :128], block[:, 128:]))
    if first:
        comp, peer_keys, peer_values, peer_length = (refs.pop(0) for _ in range(4))
        pairs.append(
            (
                jnp.concatenate([comp[:, :128], peer_keys[...]], axis=0),
                jnp.concatenate([comp[:, 128:], peer_values[...]], axis=0),
            )
        )
    else:
        acc_in, stats_in = refs.pop(0), refs.pop(0)
    out = refs.pop(0)
    win = q_own.shape[0]
    rows = 2 * win
    if first:
        row = lax.broadcasted_iota(jnp.int32, (rows, rows), 0)
        slot = lax.broadcasted_iota(jnp.int32, (rows, rows), 1)
        far_slot = (slot - win).astype(jnp.float32)
        bound = peer_length[0:1, 0:1].astype(jnp.float32)
        own = (row < win) & (slot <= row) & (slot < length[0])
        peer = (row >= win) & (slot >= win) & (slot <= row) & (far_slot < bound)
        seen = own | peer

    def score(h):
        cols = slice(h * 128, h * 128 + 128)
        q = jnp.concatenate([q_own[:, cols], q_peer[:, cols]], axis=0)
        scores = [
            lax.dot_general(
                q, keys, (((1,), (1,)), ((), ())), preferred_element_type=jnp.float32
            )
            for keys, _ in pairs
        ]
        if first:
            scores[-1] = jnp.where(seen, scores[-1], -jnp.inf)
        return scores

    if not last:
        lane = lax.broadcasted_iota(jnp.int32, (rows, 128), 1)
        found = jnp.zeros((rows, 128), jnp.float32)
    ahead = score(0)
    for h in range(heads):
        cols = slice(h * 128, h * 128 + 128)
        scores = ahead
        if h + 1 < heads:
            ahead = score(h + 1)
        peak = None
        for block in scores:
            for j in range(0, block.shape[1], 128):
                piece = block[:, j : j + 128]
                peak = piece if peak is None else jnp.maximum(peak, piece)
        top = jnp.max(peak, axis=-1, keepdims=True)
        if not first:
            old = stats_in[:, h : h + 1]
            top = jnp.maximum(top, old)
            factor = jnp.exp2((old - top) * scale)
        acc = None
        for block, (_, values) in zip(scores, pairs):
            weights = jnp.exp2((block - top) * scale).astype(jnp.bfloat16)
            wide = jnp.concatenate([values, jnp.ones_like(values)], axis=1)
            part = jnp.dot(weights, wide, preferred_element_type=jnp.float32)
            acc = part if acc is None else acc + part
        summed, total = acc[:, :128], acc[:, 128:]
        if not first:
            summed = summed + acc_in[:, cols] * factor
            total = total + stats_in[:, heads + h : heads + h + 1] * factor
        if last:
            out[:, cols] = (summed / total).astype(jnp.bfloat16)
        else:
            out[:, cols] = summed
            found = jnp.where(lane == h, top, found)
            found = jnp.where(lane == heads + h, total, found)
    if not last:
        refs[0][...] = found


def attend(length, q_own, pair, blocks, scale, comp=None, state=None, last=False):
    heads = HEADS
    win, width = q_own.shape
    rows = 2 * win
    steps = width // (128 * heads)
    columns = width // 128
    operands = list(blocks)
    specs = [pl.BlockSpec(b.shape, lambda s: (0, 0)) for b in blocks]
    if comp is not None:
        operands += [comp, pair, pair, pair]
        specs.append(pl.BlockSpec(comp.shape, lambda s: (0, 0)))
        for offset in range(3):
            specs.append(pl.BlockSpec((win, 128), lambda s, o=offset: (0, columns + o)))
    else:
        operands += state
        specs += [
            pl.BlockSpec((rows, 128 * heads), lambda s: (0, s)),
            pl.BlockSpec((rows, 128), lambda s: (0, s)),
        ]
    qspec = pl.BlockSpec((win, 128 * heads), lambda s: (0, s))
    keys = sum(b.shape[0] for b in blocks)
    out_specs = [pl.BlockSpec((rows, 128 * heads), lambda s: (0, s))]
    out_shape = [jax.ShapeDtypeStruct((rows, width), jnp.bfloat16 if last else jnp.float32)]
    if not last:
        out_specs.append(pl.BlockSpec((rows, 128), lambda s: (0, s)))
        out_shape.append(jax.ShapeDtypeStruct((rows, 128 * steps), jnp.float32))
    return pl.pallas_call(
        functools.partial(
            attend_kernel,
            scale=scale,
            heads=heads,
            count=len(blocks),
            first=comp is not None,
            last=last,
        ),
        grid=(steps,),
        in_specs=[pl.BlockSpec(memory_space=pltpu.SMEM), qspec, qspec] + specs,
        out_specs=out_specs,
        out_shape=out_shape,
        compiler_params=pltpu.CompilerParams(vmem_limit_bytes=VMEM),
        cost_estimate=pl.CostEstimate(
            flops=rows * columns * keys * 128 * 8,
            bytes_accessed=4 * 2**20,
            transcendentals=rows * columns * keys,
        ),
    )(length, q_own, pair, *operands)


def project_kernel(order, plane, attended, weight, out, *rest, arrange):
    rows, features = attended.shape
    if arrange:
        placed, step = rest[0], pl.program_id(0)

        @pl.when(step == 0)
        def _():
            row = lax.broadcasted_iota(jnp.int32, (256, 1), 0)
            column = lax.broadcasted_iota(jnp.int32, (256, features), 1)
            total = None
            for pair in range(features // 256):
                head = 2 * pair + row // 128
                feature = row % 128
                other = (feature // 64) ^ plane[0]
                target = (feature % 64) // 2 * 32 + other * 16 + head * 2 + feature % 2
                place = jnp.where(column == target, 1.0, 0.0).astype(jnp.bfloat16)
                part = jnp.dot(
                    attended[:, 256 * pair : 256 * pair + 256],
                    place,
                    preferred_element_type=jnp.float32,
                )
                total = part if total is None else total + part
            placed[...] = total.astype(jnp.bfloat16)

        attended = placed
    out[0] = jnp.dot(
        attended[...], weight[...], preferred_element_type=jnp.float32
    ).astype(jnp.bfloat16)


def project(order, plane, attended, weight, arrange):
    rows, features = attended.shape
    block = weight.shape[1] // 4
    whole = pl.BlockSpec((rows, features), lambda s, order, plane: (0, 0))
    out_specs = [pl.BlockSpec((1, rows, block), lambda s, order, plane: (s, 0, 0))]
    out_shape = [jax.ShapeDtypeStruct((2, rows, block), jnp.bfloat16)]
    if arrange:
        out_specs.append(whole)
        out_shape.append(jax.ShapeDtypeStruct((rows, features), jnp.bfloat16))
    return pl.pallas_call(
        functools.partial(project_kernel, arrange=arrange),
        grid_spec=pltpu.PrefetchScalarGridSpec(
            num_scalar_prefetch=2,
            grid=(2,),
            in_specs=[
                whole,
                pl.BlockSpec((features, block), lambda s, order, plane: (0, order[s])),
            ],
            out_specs=out_specs,
        ),
        out_shape=out_shape,
        compiler_params=pltpu.CompilerParams(vmem_limit_bytes=VMEM),
        cost_estimate=pl.CostEstimate(
            flops=4 * rows * features * block,
            bytes_accessed=6 * 2**20,
            transcendentals=0,
        ),
    )(order, plane, attended, weight)


def per_device(
    queries, comp_keys, comp_values, prompt_keys, prompt_values, page_table, lengths, out_weight
):
    win = queries.shape[0]
    head_size = 128
    heads = queries.shape[1] // head_size
    page = prompt_keys.shape[0]
    seq_count = XL * NZ * NY
    width = out_weight.shape[2]
    plane = lax.axis_index("seq") // (NZ * NY)
    tp_index = lax.axis_index("tp")
    core, far = tp_index % 2, tp_index // 2
    slots = jnp.arange(win, dtype=jnp.int32)

    halves = out_weight.reshape(2, heads, width)
    hold = jnp.where(plane == 0, halves[0], halves[1])
    pass_on = jnp.where(plane == 0, halves[1], halves[0])
    rows = jnp.concatenate([hold, across(pass_on)], axis=0)
    groups = [[seq_id(x, 0, 0) + i for i in range(NZ * NY)] for x in range(XL)]
    weight = lax.all_gather(rows, "seq", axis=0, tiled=True, axis_index_groups=groups)

    positions = jnp.concatenate(
        [page * seq_count + slots, page_table[0] * page + jnp.arange(page, dtype=jnp.int32)]
    )
    which = plane.reshape(1).astype(jnp.int32)
    q_own, pair, comp, kv, kv_give = prepare(
        which,
        lengths,
        *tables(positions, head_size),
        queries,
        comp_keys,
        comp_values,
        prompt_keys,
        prompt_values,
    )

    kv = jnp.concatenate([kv, across(kv_give)], axis=0)
    near = jnp.concatenate([kv] + [along_y(kv, k) for k in range(1, NY)], axis=0)
    pair = across(pair)

    scale = LOG2E / math.sqrt(head_size)
    run = functools.partial(attend, lengths, q_own, pair, scale=scale)
    up1, down1 = along_z(near, 1), along_z(near, -1)
    up2, down2 = along_z(up1, 1), along_z(down1, -1)
    state = run([near, up1, down1], comp=comp)
    up3, down3 = along_z(up2, 1), along_z(down2, -1)
    state = run([up2, down2], state=state)
    half = near.shape[0] // 2
    up4, down4 = along_z(up3[:half], 1), along_z(down3[half:], -1)
    state = run([up3, down3], state=state)
    (attended,) = run([up4, down4], state=state, last=True)

    give_order = jnp.stack([2 * far + 1 - core, 2 * (1 - far) + 1 - core]).astype(jnp.int32)
    keep_order = jnp.stack([2 * far + core, 2 * (1 - far) + core]).astype(jnp.int32)
    give, placed = project(give_order, which, attended, weight, True)
    came = lax.ppermute(give, "tp", [(0, 1), (1, 0), (2, 3), (3, 2)])
    (keep,) = project(keep_order, which, placed, weight, False)

    chip = (keep.astype(jnp.float32) + came.astype(jnp.float32)).astype(jnp.bfloat16)
    axes = ("seq", "tp")
    one = lax.ppermute(chip[1, :win], axes, both_perm(0, 2))
    two = lax.ppermute(chip[0, win:], axes, both_perm(1, 0))
    three = lax.ppermute(chip[1, win:], axes, both_perm(1, 2))
    result = chip[0, :win].astype(jnp.float32) + two.astype(jnp.float32)
    result = result + one.astype(jnp.float32) + three.astype(jnp.float32)
    return jnp.where((slots < lengths[0])[:, None], result, 0.0).astype(jnp.bfloat16)


def solution(mesh):
    in_specs = (
        P("seq", "tp"),
        P("seq", "tp"),
        P("seq", "tp"),
        P("seq", "tp"),
        P("seq", "tp"),
        P("seq"),
        P("seq"),
        P("tp", "seq", None),
    )
    out_specs = P("seq", "tp")
    return jax.shard_map(
        per_device, mesh=mesh, in_specs=in_specs, out_specs=out_specs, check_vma=False
    )
```

```python
import functools
import math

import jax
import jax.numpy as jnp
from jax import lax
from jax.experimental import pallas as pl
from jax.experimental.pallas import tpu as pltpu
from jax.sharding import PartitionSpec as P

theta_base = 1000000.0
XL, NZ, NY = 2, 8, 4
LOG2E = math.log2(math.e)
MIB = 2**20
HEADS = 4
CUT = 256


def seq_id(x, z, y):
    return ((x % XL) * NZ + z % NZ) * NY + y % NY


def seq_perm(dx, dz, dy):
    return [
        (seq_id(x, z, y), seq_id(x + dx, z + dz, y + dy))
        for x in range(XL)
        for z in range(NZ)
        for y in range(NY)
    ]


def both_perm(dx, dt):
    return [
        (4 * seq_id(x, z, y) + t, 4 * seq_id(x + dx, z, y) + t ^ dt)
        for x in range(XL)
        for z in range(NZ)
        for y in range(NY)
        for t in range(4)
    ]


def along_z(x, k):
    return lax.ppermute(x, "seq", seq_perm(0, k, 0))


def along_y(x, k):
    return lax.ppermute(x, "seq", seq_perm(0, 0, k))


def across(x):
    return lax.ppermute(x, "seq", seq_perm(1, 0, 0))


def tables(positions, size):
    half = size // 2
    freq = jnp.power(
        jnp.float32(theta_base), -2.0 * jnp.arange(half, dtype=jnp.float32) / size
    )
    angle = positions.astype(jnp.float32)[:, None] * freq[None, :]
    return jnp.cos(angle), jnp.sin(angle)


def ring(block, move, count):
    up = down = block
    pieces = [block]
    for _ in range(1, count // 2):
        up, down = move(up, 1), move(down, -1)
        pieces += [up, down]
    half = block.shape[0] // 2
    return pieces + [move(up[:half], 1), move(down[half:], -1)]


def prepare_kernel(
    plane, length, cosines, sines, q_own, q_give, ck_own, ck_give, cv_own, cv_give,
    pk_own, pk_give, pv_own, pv_give, w_own, w_give, q_out, pair_out, comp_out, own_out, give_out,
):
    win = q_own.shape[0]

    def table(rows):
        cosine, sine = cosines[rows, :], sines[rows, :]
        return (
            jnp.concatenate([cosine, cosine], axis=1),
            jnp.concatenate([-sine, sine], axis=1),
        )

    def turn(block, cosine, sine):
        block = block.astype(jnp.float32)
        return (block * cosine + pltpu.roll(block, 64, 1) * sine).astype(jnp.bfloat16)

    qc, qs = table(slice(0, win))
    kc, ks = table(slice(win, None))
    for out, keys, values, weight in (
        (give_out, pk_give, pv_give, w_give),
        (own_out, pk_own, pv_own, w_own),
    ):
        count = win // 16
        turned = turn(keys[...], kc, ks)
        for g in range(count):
            rows = slice(16 * g, 16 * g + 16)
            out[:, 256 * g : 256 * g + 128] = turned[rows]
            out[:, 256 * g + 128 : 256 * g + 256] = values[rows, :]
        block = weight.shape[2] // 4
        base = 256 * count
        for t in range(4):
            cols = base + t * CUT
            out[:, cols : cols + CUT] = weight[0, :, t * block : t * block + CUT]
            cols = base + 4 * CUT + t * (block - CUT)
            out[:, cols : cols + block - CUT] = weight[0, :, t * block + CUT : (t + 1) * block]
    comp_out[:, :128] = turn(ck_own[...], qc, qs)
    comp_out[:, 128:] = cv_own[...]
    width = q_own.shape[1]
    for h in range(width // 128):
        cols = slice(h * 128, h * 128 + 128)
        q_out[:, cols] = turn(q_own[:, cols], qc, qs)
        pair_out[:, cols] = turn(q_give[:, cols], qc, qs)
    pair_out[:, width : width + 128] = turn(ck_give[...], qc, qs)
    pair_out[:, width + 128 : width + 256] = cv_give[...]
    pair_out[:, width + 256 :] = jnp.full(
        (win, 128), length[0].astype(jnp.float32), jnp.float32
    ).astype(jnp.bfloat16)


def prepare(plane, length, cosines, sines, q, ckey, cval, pkey, pval, weight):
    win, width = q.shape[0], q.shape[1] // 2
    whole = pl.BlockSpec(cosines.shape, lambda s, p, n: (0, 0))
    specs, operands = [whole, whole], [cosines, sines]
    for array in (q, ckey, cval, pkey, pval):
        shape = (array.shape[0], array.shape[1] // 2)
        specs += [
            pl.BlockSpec(shape, lambda s, p, n: (0, p[0])),
            pl.BlockSpec(shape, lambda s, p, n: (0, 1 - p[0])),
        ]
        operands += [array, array]
    shape = (1,) + weight.shape[1:]
    specs += [
        pl.BlockSpec(shape, lambda s, p, n: (p[0], 0, 0)),
        pl.BlockSpec(shape, lambda s, p, n: (1 - p[0], 0, 0)),
    ]
    operands += [weight, weight]
    cross = (16, 256 * (win // 16) + weight.shape[2])
    shapes = [(win, width), (win, width + 384), (win, 256), cross, cross]
    return pl.pallas_call(
        prepare_kernel,
        grid_spec=pltpu.PrefetchScalarGridSpec(
            num_scalar_prefetch=2,
            grid=(1,),
            in_specs=specs,
            out_specs=[pl.BlockSpec(shape, lambda s, p, n: (0, 0)) for shape in shapes],
        ),
        out_shape=[jax.ShapeDtypeStruct(shape, jnp.bfloat16) for shape in shapes],
        compiler_params=pltpu.CompilerParams(vmem_limit_bytes=56 * MIB),
    )(plane, length, *operands)


def attend_kernel(length, q_own, q_peer, *refs, scale, heads, count, first, last):
    refs = list(refs)
    pairs = []
    for _ in range(count):
        block = refs.pop(0)
        span = 256 * max(1, 256 // block.shape[0])
        for start in range(0, block.shape[1], span):
            groups = range(start, start + span, 256)
            pairs.append(
                (
                    jnp.concatenate([block[:, g : g + 128] for g in groups], axis=0),
                    jnp.concatenate([block[:, g + 128 : g + 256] for g in groups], axis=0),
                )
            )
    if first:
        comp, peer_keys, peer_values, peer_length = (refs.pop(0) for _ in range(4))
        pairs.append(
            (
                jnp.concatenate([comp[:, :128], peer_keys[...]], axis=0),
                jnp.concatenate([comp[:, 128:], peer_values[...]], axis=0),
            )
        )
    else:
        acc_in, stats_in = refs.pop(0), refs.pop(0)
    out = refs.pop(0)
    win = q_own.shape[0]
    rows = 2 * win
    if first:
        row = lax.broadcasted_iota(jnp.int32, (rows, rows), 0)
        slot = lax.broadcasted_iota(jnp.int32, (rows, rows), 1)
        far_slot = (slot - win).astype(jnp.float32)
        bound = peer_length[0:1, 0:1].astype(jnp.float32)
        own = (row < win) & (slot <= row) & (slot < length[0])
        peer = (row >= win) & (slot >= win) & (slot <= row) & (far_slot < bound)
        seen = own | peer

    def score(h):
        cols = slice(h * 128, h * 128 + 128)
        q = jnp.concatenate([q_own[:, cols], q_peer[:, cols]], axis=0)
        scores = [
            lax.dot_general(
                q, keys, (((1,), (1,)), ((), ())), preferred_element_type=jnp.float32
            )
            for keys, _ in pairs
        ]
        if first:
            scores[-1] = jnp.where(seen, scores[-1], -jnp.inf)
        return scores

    if not last:
        lane = lax.broadcasted_iota(jnp.int32, (rows, 128), 1)
        found = jnp.zeros((rows, 128), jnp.float32)
    ahead = score(0)
    for h in range(heads):
        cols = slice(h * 128, h * 128 + 128)
        scores = ahead
        if h + 1 < heads:
            ahead = score(h + 1)
        peak = None
        for block in scores:
            for j in range(0, block.shape[1], 128):
                piece = block[:, j : j + 128]
                peak = piece if peak is None else jnp.maximum(peak, piece)
        top = jnp.max(peak, axis=-1, keepdims=True)
        if not first:
            old = stats_in[:, h : h + 1]
            top = jnp.maximum(top, old)
            factor = jnp.exp2((old - top) * scale)
        acc = None
        for block, (_, values) in zip(scores, pairs):
            weights = jnp.exp2((block - top) * scale).astype(jnp.bfloat16)
            wide = jnp.concatenate([values, jnp.ones_like(values)], axis=1)
            part = jnp.dot(weights, wide, preferred_element_type=jnp.float32)
            acc = part if acc is None else acc + part
        summed, total = acc[:, :128], acc[:, 128:]
        if not first:
            summed = summed + acc_in[:, cols] * factor
            total = total + stats_in[:, heads + h : heads + h + 1] * factor
        if last:
            out[:, cols] = (summed / total).astype(jnp.bfloat16)
        else:
            out[:, cols] = summed
            found = jnp.where(lane == h, top, found)
            found = jnp.where(lane == heads + h, total, found)
    if not last:
        refs[0][...] = found


def attend(length, q_own, pair, blocks, scale, comp=None, state=None, last=False):
    heads = HEADS
    win, width = q_own.shape
    rows = 2 * win
    steps = width // (128 * heads)
    columns = width // 128
    operands = list(blocks)
    lanes = 256 * (win // 16)
    specs = [pl.BlockSpec((b.shape[0], lanes), lambda s: (0, 0)) for b in blocks]
    if comp is not None:
        operands += [comp, pair, pair, pair]
        specs.append(pl.BlockSpec(comp.shape, lambda s: (0, 0)))
        for offset in range(3):
            specs.append(pl.BlockSpec((win, 128), lambda s, o=offset: (0, columns + o)))
    else:
        operands += state
        specs += [
            pl.BlockSpec((rows, 128 * heads), lambda s: (0, s)),
            pl.BlockSpec((rows, 128), lambda s: (0, s)),
        ]
    qspec = pl.BlockSpec((win, 128 * heads), lambda s: (0, s))
    keys = sum(b.shape[0] * lanes // 256 for b in blocks)
    out_specs = [pl.BlockSpec((rows, 128 * heads), lambda s: (0, s))]
    out_shape = [jax.ShapeDtypeStruct((rows, width), jnp.bfloat16 if last else jnp.float32)]
    if not last:
        out_specs.append(pl.BlockSpec((rows, 128), lambda s: (0, s)))
        out_shape.append(jax.ShapeDtypeStruct((rows, 128 * steps), jnp.float32))
    return pl.pallas_call(
        functools.partial(
            attend_kernel,
            scale=scale,
            heads=heads,
            count=len(blocks),
            first=comp is not None,
            last=last,
        ),
        grid=(steps,),
        in_specs=[pl.BlockSpec(memory_space=pltpu.SMEM), qspec, qspec] + specs,
        out_specs=out_specs,
        out_shape=out_shape,
        compiler_params=pltpu.CompilerParams(vmem_limit_bytes=30 * MIB),
        cost_estimate=pl.CostEstimate(
            flops=rows * columns * keys * 128 * 8,
            bytes_accessed=4 * 2**20,
            transcendentals=rows * columns * keys,
        ),
    )(length, q_own, pair, *operands)


def project_kernel(place, *refs, count, arrange):
    refs = list(refs)
    ins = [refs.pop(0) for _ in range(1 if arrange else 2)]
    weights = [[refs.pop(0) for _ in range(n)] for n in count]
    out = refs.pop(0)
    if arrange:
        (attended,), ins = ins, refs
        features = attended.shape[1]

        @pl.when(pl.program_id(0) == 0)
        def _():
            row = lax.broadcasted_iota(jnp.int32, (256, 1), 0)
            column = lax.broadcasted_iota(jnp.int32, (256, features), 1)
            plane, z, y = place[0], place[1], place[2]
            totals = [None, None]
            for pair in range(features // 256):
                head = 2 * pair + row // 128
                feature = row % 128
                other = (feature // 64) ^ plane
                dz = (feature // 8 % NZ + NZ - z) % NZ
                dy = (feature // 2 % NY + NY - y) % NY
                z_at = jnp.where(dz < NZ // 2, 2 * dz, 2 * NZ - 1 - 2 * dz)
                y_ring = jnp.where(dy < NY // 2, 2 * dy, 2 * NY - 1 - 2 * dy)
                y_sent = (NY - dy) % NY
                within = other * 16 + head * 2 + feature % 2
                targets = (
                    (y_ring * NZ + z_at) * 32 + within,
                    (z_at * NY + y_sent) * 32 + within,
                )
                block = attended[:, 256 * pair : 256 * pair + 256]
                for k, target in enumerate(targets):
                    moved = jnp.where(column == target, 1.0, 0.0).astype(jnp.bfloat16)
                    part = jnp.dot(block, moved, preferred_element_type=jnp.float32)
                    totals[k] = part if totals[k] is None else totals[k] + part
            for total, ref in zip(totals, ins):
                ref[...] = total.astype(jnp.bfloat16)

    start = 0
    for rows, pieces in zip(ins, weights):
        weight = jnp.concatenate([p[...] for p in pieces], axis=0)
        width = weight.shape[1]
        out[0, :, start : start + width] = jnp.dot(
            rows[...], weight, preferred_element_type=jnp.float32
        ).astype(jnp.bfloat16)
        start += width


def project(place, ins, first, second, offset):
    arrange = len(ins) == 1
    rows, features = ins[0].shape
    rest = second[0].shape[1] // 4
    block = CUT + rest
    whole = pl.BlockSpec((rows, features), lambda s, at: (0, 0))

    def column(s, at):
        return 2 * (at[4] ^ s) + (1 - at[3] if arrange else at[3])

    specs = [whole] * len(ins)
    for p in first:
        specs.append(
            pl.BlockSpec((p.shape[0], CUT), lambda s, at: (0, offset // CUT + column(s, at)))
        )
    for p in second:
        specs.append(pl.BlockSpec((p.shape[0], rest), lambda s, at: (0, column(s, at))))
    out_specs = [pl.BlockSpec((1, rows, block), lambda s, at: (s, 0, 0))]
    out_shape = [jax.ShapeDtypeStruct((2, rows, block), jnp.bfloat16)]
    if arrange:
        out_specs += [whole, whole]
        out_shape += [jax.ShapeDtypeStruct((rows, features), jnp.bfloat16)] * 2
    return pl.pallas_call(
        functools.partial(project_kernel, count=(len(first), len(second)), arrange=arrange),
        grid_spec=pltpu.PrefetchScalarGridSpec(
            num_scalar_prefetch=1, grid=(2,), in_specs=specs, out_specs=out_specs
        ),
        out_shape=out_shape,
        compiler_params=pltpu.CompilerParams(vmem_limit_bytes=20 * MIB),
        cost_estimate=pl.CostEstimate(
            flops=4 * rows * features * block,
            bytes_accessed=6 * 2**20,
            transcendentals=0,
        ),
    )(place, *ins, *first, *second)


def per_device(
    queries, comp_keys, comp_values, prompt_keys, prompt_values, page_table, lengths, out_weight
):
    win = queries.shape[0]
    head_size = 128
    heads = queries.shape[1] // head_size
    page = prompt_keys.shape[0]
    seq_count = XL * NZ * NY
    width = out_weight.shape[2]
    seq_index = lax.axis_index("seq")
    tp_index = lax.axis_index("tp")
    place = jnp.stack(
        [seq_index // (NZ * NY), seq_index // NY % NZ, seq_index % NY, tp_index % 2, tp_index // 2]
    ).astype(jnp.int32)
    slots = jnp.arange(win, dtype=jnp.int32)

    positions = jnp.concatenate(
        [page * seq_count + slots, page_table[0] * page + jnp.arange(page, dtype=jnp.int32)]
    )
    q_own, pair, comp, own, give = prepare(
        place[:1],
        lengths,
        *tables(positions, head_size),
        queries,
        comp_keys,
        comp_values,
        prompt_keys,
        prompt_values,
        out_weight.reshape(2, heads, width),
    )
    both = jnp.concatenate([own, across(give)], axis=0)

    lanes = 256 * (win // 16)
    cut = lanes + 4 * CUT
    first, second = both[:, :cut], both[:, cut:]
    up = down = first
    pieces = [first]
    for hop in range(1, NZ // 2):
        up, down = along_z(up, 1), along_z(down, -1)
        pieces += [up, down]
        if hop == 2:
            up, down, second = lax.optimization_barrier((up, down, second))
            second = [second] + [along_y(second, k) for k in range(1, NY)]
    half = first.shape[0] // 2
    pieces += [along_z(up[:half], 1), along_z(down[half:], -1)]
    first, second = jnp.concatenate(pieces, axis=0), jnp.concatenate(second, axis=0)

    first, second, pair = lax.optimization_barrier((first, second, pair))
    scale = LOG2E / math.sqrt(head_size)
    run = functools.partial(attend, lengths, q_own, across(pair), scale=scale)
    half = first.shape[0] // 2
    y_up, y_down = along_y(first, 1), along_y(first, -1)
    z_up, z_down = along_z(second, 1), along_z(second, -1)
    state = run([first], comp=comp)
    z_up, z_down, state = lax.optimization_barrier((z_up, z_down, state))
    first, second = [first, y_up, y_down], [second, z_up, z_down]
    first += [along_y(y_up[:half], 1), along_y(y_down[half:], -1)]
    z_up, z_down = along_z(z_up, 1), along_z(z_down, -1)
    z_up, z_down, state = lax.optimization_barrier((z_up, z_down, state))
    second += [z_up, z_down]
    state = run(first[1:3], state=state)
    z_up, z_down = along_z(z_up, 1), along_z(z_down, -1)
    second += [z_up, z_down]
    half = z_up.shape[0] // 2
    second += [along_z(z_up[:half], 1), along_z(z_down[half:], -1)]
    (attended,) = run(first[3:], state=state, last=True)

    give, *placed = project(place, [attended], first, second, lanes)
    came = lax.ppermute(give, "tp", [(0, 1), (1, 0), (2, 3), (3, 2)])
    (keep,) = project(place, placed, first, second, lanes)

    chip = (keep.astype(jnp.float32) + came.astype(jnp.float32)).astype(jnp.bfloat16)
    axes = ("seq", "tp")
    one = lax.ppermute(chip[1, :win], axes, both_perm(0, 2))
    two = lax.ppermute(chip[0, win:], axes, both_perm(1, 0))
    three = lax.ppermute(chip[1, win:], axes, both_perm(1, 2))
    result = chip[0, :win].astype(jnp.float32) + two.astype(jnp.float32)
    result = result + one.astype(jnp.float32) + three.astype(jnp.float32)
    return jnp.where((slots < lengths[0])[:, None], result, 0.0).astype(jnp.bfloat16)


def solution(mesh):
    in_specs = (
        P("seq", "tp"),
        P("seq", "tp"),
        P("seq", "tp"),
        P("seq", "tp"),
        P("seq", "tp"),
        P("seq"),
        P("seq"),
        P("tp", "seq", None),
    )
    out_specs = P("seq", "tp")
    return jax.shard_map(
        per_device, mesh=mesh, in_specs=in_specs, out_specs=out_specs, check_vma=False
    )
```

```python
import functools
import math

import jax
import jax.numpy as jnp
from jax import lax
from jax.experimental import pallas as pl
from jax.experimental.pallas import tpu as pltpu
from jax.sharding import PartitionSpec as P

theta_base = 1000000.0
XL, NZ, NY = 2, 8, 4
LOG2E = math.log2(math.e)
MIB = 2**20
HEADS = 4
CUT = 256


def seq_id(x, z, y):
    return ((x % XL) * NZ + z % NZ) * NY + y % NY


def seq_perm(dx, dz, dy):
    return [
        (seq_id(x, z, y), seq_id(x + dx, z + dz, y + dy))
        for x in range(XL)
        for z in range(NZ)
        for y in range(NY)
    ]


def both_perm(dx, dt):
    return [
        (4 * seq_id(x, z, y) + t, 4 * seq_id(x + dx, z, y) + t ^ dt)
        for x in range(XL)
        for z in range(NZ)
        for y in range(NY)
        for t in range(4)
    ]


def along_z(x, k):
    return lax.ppermute(x, "seq", seq_perm(0, k, 0))


def along_y(x, k):
    return lax.ppermute(x, "seq", seq_perm(0, 0, k))


def across(x):
    return lax.ppermute(x, "seq", seq_perm(1, 0, 0))


def tables(positions, size):
    half = size // 2
    freq = jnp.power(
        jnp.float32(theta_base), -2.0 * jnp.arange(half, dtype=jnp.float32) / size
    )
    angle = positions.astype(jnp.float32)[:, None] * freq[None, :]
    return jnp.cos(angle), jnp.sin(angle)


def ring(block, move, count):
    up = down = block
    pieces = [block]
    for _ in range(1, count // 2):
        up, down = move(up, 1), move(down, -1)
        pieces += [up, down]
    half = block.shape[0] // 2
    return pieces + [move(up[:half], 1), move(down[half:], -1)]


def prepare_kernel(
    plane, length, cosines, sines, q_own, q_give, ck_own, ck_give, cv_own, cv_give,
    pk_own, pk_give, pv_own, pv_give, w_own, w_give, q_out, pair_out, comp_out, own_out, give_out,
):
    win = q_own.shape[0]

    def table(rows):
        cosine, sine = cosines[rows, :], sines[rows, :]
        return (
            jnp.concatenate([cosine, cosine], axis=1),
            jnp.concatenate([-sine, sine], axis=1),
        )

    def turn(block, cosine, sine):
        block = block.astype(jnp.float32)
        return (block * cosine + pltpu.roll(block, 64, 1) * sine).astype(jnp.bfloat16)

    qc, qs = table(slice(0, win))
    kc, ks = table(slice(win, None))
    for out, keys, values, weight in (
        (give_out, pk_give, pv_give, w_give),
        (own_out, pk_own, pv_own, w_own),
    ):
        count = win // 16
        turned = turn(keys[...], kc, ks)
        for g in range(count):
            rows = slice(16 * g, 16 * g + 16)
            out[:, 256 * g : 256 * g + 128] = turned[rows]
            out[:, 256 * g + 128 : 256 * g + 256] = values[rows, :]
        block = weight.shape[2] // 4
        base = 256 * count
        for t in range(4):
            cols = base + t * CUT
            out[:, cols : cols + CUT] = weight[0, :, t * block : t * block + CUT]
            cols = base + 4 * CUT + t * (block - CUT)
            out[:, cols : cols + block - CUT] = weight[0, :, t * block + CUT : (t + 1) * block]
    comp_out[:, :128] = turn(ck_own[...], qc, qs)
    comp_out[:, 128:] = cv_own[...]
    width = q_own.shape[1]
    for h in range(width // 128):
        cols = slice(h * 128, h * 128 + 128)
        q_out[:, cols] = turn(q_own[:, cols], qc, qs)
        pair_out[:, cols] = turn(q_give[:, cols], qc, qs)
    pair_out[:, width : width + 128] = turn(ck_give[...], qc, qs)
    pair_out[:, width + 128 : width + 256] = cv_give[...]
    pair_out[:, width + 256 :] = jnp.full(
        (win, 128), length[0].astype(jnp.float32), jnp.float32
    ).astype(jnp.bfloat16)


def prepare(plane, length, cosines, sines, q, ckey, cval, pkey, pval, weight):
    win, width = q.shape[0], q.shape[1] // 2
    whole = pl.BlockSpec(cosines.shape, lambda s, p, n: (0, 0))
    specs, operands = [whole, whole], [cosines, sines]
    for array in (q, ckey, cval, pkey, pval):
        shape = (array.shape[0], array.shape[1] // 2)
        specs += [
            pl.BlockSpec(shape, lambda s, p, n: (0, p[0])),
            pl.BlockSpec(shape, lambda s, p, n: (0, 1 - p[0])),
        ]
        operands += [array, array]
    shape = (1,) + weight.shape[1:]
    specs += [
        pl.BlockSpec(shape, lambda s, p, n: (p[0], 0, 0)),
        pl.BlockSpec(shape, lambda s, p, n: (1 - p[0], 0, 0)),
    ]
    operands += [weight, weight]
    cross = (16, 256 * (win // 16) + weight.shape[2])
    shapes = [(win, width), (win, width + 384), (win, 256), cross, cross]
    return pl.pallas_call(
        prepare_kernel,
        grid_spec=pltpu.PrefetchScalarGridSpec(
            num_scalar_prefetch=2,
            grid=(1,),
            in_specs=specs,
            out_specs=[pl.BlockSpec(shape, lambda s, p, n: (0, 0)) for shape in shapes],
        ),
        out_shape=[jax.ShapeDtypeStruct(shape, jnp.bfloat16) for shape in shapes],
        compiler_params=pltpu.CompilerParams(vmem_limit_bytes=56 * MIB),
    )(plane, length, *operands)


def attend_kernel(length, q_own, q_peer, *refs, scale, heads, count, first, last):
    refs = list(refs)
    pairs = []
    for _ in range(count):
        block = refs.pop(0)
        span = 256 * max(1, 256 // block.shape[0])
        for start in range(0, block.shape[1], span):
            groups = range(start, start + span, 256)
            pairs.append(
                (
                    jnp.concatenate([block[:, g : g + 128] for g in groups], axis=0),
                    jnp.concatenate([block[:, g + 128 : g + 256] for g in groups], axis=0),
                )
            )
    if first:
        comp, peer_keys, peer_values, peer_length = (refs.pop(0) for _ in range(4))
        pairs.append(
            (
                jnp.concatenate([comp[:, :128], peer_keys[...]], axis=0),
                jnp.concatenate([comp[:, 128:], peer_values[...]], axis=0),
            )
        )
    else:
        acc_in, stats_in = refs.pop(0), refs.pop(0)
    out = refs.pop(0)
    win = q_own.shape[0]
    rows = 2 * win
    if first:
        row = lax.broadcasted_iota(jnp.int32, (rows, rows), 0)
        slot = lax.broadcasted_iota(jnp.int32, (rows, rows), 1)
        far_slot = (slot - win).astype(jnp.float32)
        bound = peer_length[0:1, 0:1].astype(jnp.float32)
        own = (row < win) & (slot <= row) & (slot < length[0])
        peer = (row >= win) & (slot >= win) & (slot <= row) & (far_slot < bound)
        seen = own | peer

    def score(h):
        cols = slice(h * 128, h * 128 + 128)
        q = jnp.concatenate([q_own[:, cols], q_peer[:, cols]], axis=0)
        scores = [
            lax.dot_general(
                q, keys, (((1,), (1,)), ((), ())), preferred_element_type=jnp.float32
            )
            for keys, _ in pairs
        ]
        if first:
            scores[-1] = jnp.where(seen, scores[-1], -jnp.inf)
        return scores

    if not last:
        lane = lax.broadcasted_iota(jnp.int32, (rows, 128), 1)
        found = jnp.zeros((rows, 128), jnp.float32)
    ahead = score(0)
    for h in range(heads):
        cols = slice(h * 128, h * 128 + 128)
        scores = ahead
        if h + 1 < heads:
            ahead = score(h + 1)
        peak = None
        for block in scores:
            for j in range(0, block.shape[1], 128):
                piece = block[:, j : j + 128]
                peak = piece if peak is None else jnp.maximum(peak, piece)
        top = jnp.max(peak, axis=-1, keepdims=True)
        if not first:
            old = stats_in[:, h : h + 1]
            top = jnp.maximum(top, old)
            factor = jnp.exp2((old - top) * scale)
        acc = None
        for block, (_, values) in zip(scores, pairs):
            weights = jnp.exp2((block - top) * scale).astype(jnp.bfloat16)
            wide = jnp.concatenate([values, jnp.ones_like(values)], axis=1)
            part = jnp.dot(weights, wide, preferred_element_type=jnp.float32)
            acc = part if acc is None else acc + part
        summed, total = acc[:, :128], acc[:, 128:]
        if not first:
            summed = summed + acc_in[:, cols] * factor
            total = total + stats_in[:, heads + h : heads + h + 1] * factor
        if last:
            out[:, cols] = (summed / total).astype(jnp.bfloat16)
        else:
            out[:, cols] = summed
            found = jnp.where(lane == h, top, found)
            found = jnp.where(lane == heads + h, total, found)
    if not last:
        refs[0][...] = found


def attend(length, q_own, pair, blocks, scale, comp=None, state=None, last=False):
    heads = HEADS
    win, width = q_own.shape
    rows = 2 * win
    steps = width // (128 * heads)
    columns = width // 128
    operands = list(blocks)
    lanes = 256 * (win // 16)
    specs = [pl.BlockSpec((b.shape[0], lanes), lambda s: (0, 0)) for b in blocks]
    if comp is not None:
        operands += [comp, pair, pair, pair]
        specs.append(pl.BlockSpec(comp.shape, lambda s: (0, 0)))
        for offset in range(3):
            specs.append(pl.BlockSpec((win, 128), lambda s, o=offset: (0, columns + o)))
    else:
        operands += state
        specs += [
            pl.BlockSpec((rows, 128 * heads), lambda s: (0, s)),
            pl.BlockSpec((rows, 128), lambda s: (0, s)),
        ]
    qspec = pl.BlockSpec((win, 128 * heads), lambda s: (0, s))
    keys = sum(b.shape[0] * lanes // 256 for b in blocks)
    out_specs = [pl.BlockSpec((rows, 128 * heads), lambda s: (0, s))]
    out_shape = [jax.ShapeDtypeStruct((rows, width), jnp.bfloat16 if last else jnp.float32)]
    if not last:
        out_specs.append(pl.BlockSpec((rows, 128), lambda s: (0, s)))
        out_shape.append(jax.ShapeDtypeStruct((rows, 128 * steps), jnp.float32))
    return pl.pallas_call(
        functools.partial(
            attend_kernel,
            scale=scale,
            heads=heads,
            count=len(blocks),
            first=comp is not None,
            last=last,
        ),
        grid=(steps,),
        in_specs=[pl.BlockSpec(memory_space=pltpu.SMEM), qspec, qspec] + specs,
        out_specs=out_specs,
        out_shape=out_shape,
        compiler_params=pltpu.CompilerParams(vmem_limit_bytes=30 * MIB),
        cost_estimate=pl.CostEstimate(
            flops=rows * columns * keys * 128 * 8,
            bytes_accessed=4 * 2**20,
            transcendentals=rows * columns * keys,
        ),
    )(length, q_own, pair, *operands)


def project_kernel(place, *refs, count, arrange):
    refs = list(refs)
    ins = [refs.pop(0) for _ in range(1 if arrange else 2)]
    weights = [[refs.pop(0) for _ in range(n)] for n in count]
    outs = [refs.pop(0), refs.pop(0)]
    if arrange:
        (attended,), ins = ins, refs
        features = attended.shape[1]

        @pl.when(pl.program_id(0) == 0)
        def _():
            row = lax.broadcasted_iota(jnp.int32, (256, 1), 0)
            column = lax.broadcasted_iota(jnp.int32, (256, features), 1)
            plane, z, y = place[0], place[1], place[2]
            totals = [None, None]
            for pair in range(features // 256):
                head = 2 * pair + row // 128
                feature = row % 128
                other = (feature // 64) ^ plane
                dz = (feature // 8 % NZ + NZ - z) % NZ
                dy = (feature // 2 % NY + NY - y) % NY
                z_at = jnp.where(dz < NZ // 2, 2 * dz, 2 * NZ - 1 - 2 * dz)
                y_ring = jnp.where(dy < NY // 2, 2 * dy, 2 * NY - 1 - 2 * dy)
                y_sent = (NY - dy) % NY
                within = other * 16 + head * 2 + feature % 2
                targets = (
                    (y_ring * NZ + z_at) * 32 + within,
                    (z_at * NY + y_sent) * 32 + within,
                )
                block = attended[:, 256 * pair : 256 * pair + 256]
                for k, target in enumerate(targets):
                    moved = jnp.where(column == target, 1.0, 0.0).astype(jnp.bfloat16)
                    part = jnp.dot(block, moved, preferred_element_type=jnp.float32)
                    totals[k] = part if totals[k] is None else totals[k] + part
            for total, ref in zip(totals, ins):
                ref[...] = total.astype(jnp.bfloat16)

    for step, out in enumerate(outs):

        @pl.when(pl.program_id(0) == step)
        def _():
            start = 0
            for rows, pieces in zip(ins, weights):
                weight = jnp.concatenate([p[...] for p in pieces], axis=0)
                width = weight.shape[1]
                out[:, start : start + width] = jnp.dot(
                    rows[...], weight, preferred_element_type=jnp.float32
                ).astype(jnp.bfloat16)
                start += width


def project(place, ins, first, second, offset, side):
    arrange = len(ins) == 1
    rows, features = ins[0].shape
    rest = second[0].shape[1] // 4
    block = CUT + rest
    whole = pl.BlockSpec((rows, features), lambda s, at: (0, 0))

    def column(s, at):
        return 2 * (at[4] ^ side) + (at[3] ^ (1 - s))

    specs = [whole] * len(ins)
    for p in first:
        specs.append(
            pl.BlockSpec((p.shape[0], CUT), lambda s, at: (0, offset // CUT + column(s, at)))
        )
    for p in second:
        specs.append(pl.BlockSpec((p.shape[0], rest), lambda s, at: (0, column(s, at))))
    out_specs = [pl.BlockSpec((rows, block), lambda s, at: (0, 0))] * 2
    out_shape = [jax.ShapeDtypeStruct((rows, block), jnp.bfloat16)] * 2
    if arrange:
        out_specs += [whole, whole]
        out_shape += [jax.ShapeDtypeStruct((rows, features), jnp.bfloat16)] * 2
    return pl.pallas_call(
        functools.partial(project_kernel, count=(len(first), len(second)), arrange=arrange),
        grid_spec=pltpu.PrefetchScalarGridSpec(
            num_scalar_prefetch=1, grid=(2,), in_specs=specs, out_specs=out_specs
        ),
        out_shape=out_shape,
        compiler_params=pltpu.CompilerParams(vmem_limit_bytes=20 * MIB),
        cost_estimate=pl.CostEstimate(
            flops=4 * rows * features * block,
            bytes_accessed=6 * 2**20,
            transcendentals=0,
        ),
    )(place, *ins, *first, *second)


def per_device(
    queries, comp_keys, comp_values, prompt_keys, prompt_values, page_table, lengths, out_weight
):
    win = queries.shape[0]
    head_size = 128
    heads = queries.shape[1] // head_size
    page = prompt_keys.shape[0]
    seq_count = XL * NZ * NY
    width = out_weight.shape[2]
    seq_index = lax.axis_index("seq")
    tp_index = lax.axis_index("tp")
    place = jnp.stack(
        [seq_index // (NZ * NY), seq_index // NY % NZ, seq_index % NY, tp_index % 2, tp_index // 2]
    ).astype(jnp.int32)
    slots = jnp.arange(win, dtype=jnp.int32)

    positions = jnp.concatenate(
        [page * seq_count + slots, page_table[0] * page + jnp.arange(page, dtype=jnp.int32)]
    )
    q_own, pair, comp, own, give = prepare(
        place[:1],
        lengths,
        *tables(positions, head_size),
        queries,
        comp_keys,
        comp_values,
        prompt_keys,
        prompt_values,
        out_weight.reshape(2, heads, width),
    )
    both = jnp.concatenate([own, across(give)], axis=0)

    lanes = 256 * (win // 16)
    cut = lanes + 4 * CUT
    first, second = both[:, :cut], both[:, cut:]
    up = down = first
    pieces = [first]
    for hop in range(1, NZ // 2):
        up, down = along_z(up, 1), along_z(down, -1)
        pieces += [up, down]
        if hop == 1:
            up, down, second, pair = lax.optimization_barrier((up, down, second, pair))
            pair = across(pair)
            second = [second] + [along_y(second, k) for k in range(1, NY)]
    half = first.shape[0] // 2
    pieces += [along_z(up[:half], 1), along_z(down[half:], -1)]
    first, second = jnp.concatenate(pieces, axis=0), jnp.concatenate(second, axis=0)

    first, second, pair = lax.optimization_barrier((first, second, pair))
    scale = LOG2E / math.sqrt(head_size)
    run = functools.partial(attend, lengths, q_own, pair, scale=scale)
    half = first.shape[0] // 2
    y_up, y_down = along_y(first, 1), along_y(first, -1)
    z_up, z_down = along_z(second, 1), along_z(second, -1)
    state = run([first], comp=comp)
    z_up, z_down, state = lax.optimization_barrier((z_up, z_down, state))
    first, second = [first, y_up, y_down], [second, z_up, z_down]
    first += [along_y(y_up[:half], 1), along_y(y_down[half:], -1)]
    z_up, z_down = along_z(z_up, 1), along_z(z_down, -1)
    z_up, z_down, state = lax.optimization_barrier((z_up, z_down, state))
    second += [z_up, z_down]
    state = run(first[1:3], state=state)
    z_up, z_down = along_z(z_up, 1), along_z(z_down, -1)
    second += [z_up, z_down]
    half = z_up.shape[0] // 2
    second += [along_z(z_up[:half], 1), along_z(z_down[half:], -1)]
    (attended,) = run(first[3:], state=state, last=True)

    def add(keep, give):
        came = lax.ppermute(give, "tp", [(0, 1), (1, 0), (2, 3), (3, 2)])
        return (keep.astype(jnp.float32) + came.astype(jnp.float32)).astype(jnp.bfloat16)

    axes = ("seq", "tp")
    give, keep, *placed = project(place, [attended], first, second, lanes, 1)
    chip = add(keep, give)
    one = lax.ppermute(chip[:win], axes, both_perm(0, 2))
    three = lax.ppermute(chip[win:], axes, both_perm(1, 2))
    give, keep = project(place, placed, first, second, lanes, 0)
    chip = add(keep, give)
    two = lax.ppermute(chip[win:], axes, both_perm(1, 0))
    result = chip[:win].astype(jnp.float32) + two.astype(jnp.float32)
    result = result + one.astype(jnp.float32) + three.astype(jnp.float32)
    return jnp.where((slots < lengths[0])[:, None], result, 0.0).astype(jnp.bfloat16)


def solution(mesh):
    in_specs = (
        P("seq", "tp"),
        P("seq", "tp"),
        P("seq", "tp"),
        P("seq", "tp"),
        P("seq", "tp"),
        P("seq"),
        P("seq"),
        P("tp", "seq", None),
    )
    out_specs = P("seq", "tp")
    return jax.shard_map(
        per_device, mesh=mesh, in_specs=in_specs, out_specs=out_specs, check_vma=False
    )
```

```python
import functools
import math

import jax
import jax.numpy as jnp
from jax import lax
from jax.experimental import pallas as pl
from jax.experimental.pallas import tpu as pltpu
from jax.sharding import PartitionSpec as P

theta_base = 1000000.0
XL, NZ, NY = 2, 8, 4
LOG2E = math.log2(math.e)
MIB = 2**20
HEADS = 4
CUT = 256


def seq_id(x, z, y):
    return ((x % XL) * NZ + z % NZ) * NY + y % NY


def seq_perm(dx, dz, dy):
    return [
        (seq_id(x, z, y), seq_id(x + dx, z + dz, y + dy))
        for x in range(XL)
        for z in range(NZ)
        for y in range(NY)
    ]


def both_perm(dx, dt):
    return [
        (4 * seq_id(x, z, y) + t, 4 * seq_id(x + dx, z, y) + t ^ dt)
        for x in range(XL)
        for z in range(NZ)
        for y in range(NY)
        for t in range(4)
    ]


def along_z(x, k):
    return lax.ppermute(x, "seq", seq_perm(0, k, 0))


def along_y(x, k):
    return lax.ppermute(x, "seq", seq_perm(0, 0, k))


def across(x):
    return lax.ppermute(x, "seq", seq_perm(1, 0, 0))


def tables(positions, size):
    half = size // 2
    freq = jnp.power(
        jnp.float32(theta_base), -2.0 * jnp.arange(half, dtype=jnp.float32) / size
    )
    angle = positions.astype(jnp.float32)[:, None] * freq[None, :]
    return jnp.cos(angle), jnp.sin(angle)


def ring(block, move, count):
    up = down = block
    pieces = [block]
    for _ in range(1, count // 2):
        up, down = move(up, 1), move(down, -1)
        pieces += [up, down]
    half = block.shape[0] // 2
    return pieces + [move(up[:half], 1), move(down[half:], -1)]


def prepare_kernel(
    plane, length, cosines, sines, q_own, q_give, ck_own, ck_give, cv_own, cv_give,
    pk_own, pk_give, pv_own, pv_give, w_own, w_give, q_out, pair_out, comp_out, own_out, give_out,
):
    win = q_own.shape[0]

    def table(rows):
        cosine, sine = cosines[rows, :], sines[rows, :]
        return (
            jnp.concatenate([cosine, cosine], axis=1),
            jnp.concatenate([-sine, sine], axis=1),
        )

    def turn(block, cosine, sine):
        block = block.astype(jnp.float32)
        return (block * cosine + pltpu.roll(block, 64, 1) * sine).astype(jnp.bfloat16)

    qc, qs = table(slice(0, win))
    kc, ks = table(slice(win, None))
    for out, keys, values, weight in (
        (give_out, pk_give, pv_give, w_give),
        (own_out, pk_own, pv_own, w_own),
    ):
        count = win // 16
        turned = turn(keys[...], kc, ks)
        for g in range(count):
            rows = slice(16 * g, 16 * g + 16)
            out[:, 256 * g : 256 * g + 128] = turned[rows]
            out[:, 256 * g + 128 : 256 * g + 256] = values[rows, :]
        rows = jnp.concatenate([weight[h] for h in range(weight.shape[0])], axis=0)
        block = weight.shape[2] // 4
        base = 256 * count
        for t in range(4):
            cols = base + t * CUT
            out[:, cols : cols + CUT] = rows[:, t * block : t * block + CUT]
            cols = base + 4 * CUT + t * (block - CUT)
            out[:, cols : cols + block - CUT] = rows[:, t * block + CUT : (t + 1) * block]
    comp_out[:, :128] = turn(ck_own[...], qc, qs)
    comp_out[:, 128:] = cv_own[...]
    width = q_own.shape[1]
    for h in range(width // 128):
        cols = slice(h * 128, h * 128 + 128)
        q_out[:, cols] = turn(q_own[:, cols], qc, qs)
        pair_out[:, cols] = turn(q_give[:, cols], qc, qs)
    pair_out[:, width : width + 128] = turn(ck_give[...], qc, qs)
    pair_out[:, width + 128 : width + 256] = cv_give[...]
    pair_out[:, width + 256 :] = jnp.full(
        (win, 128), length[0].astype(jnp.float32), jnp.float32
    ).astype(jnp.bfloat16)


def prepare(plane, length, cosines, sines, q, ckey, cval, pkey, pval, weight):
    win, width = q.shape[0], q.shape[1] // 2
    whole = pl.BlockSpec(cosines.shape, lambda s, p, n: (0, 0))
    specs, operands = [whole, whole], [cosines, sines]
    for array in (q, ckey, cval, pkey, pval):
        shape = (array.shape[0], array.shape[1] // 2)
        specs += [
            pl.BlockSpec(shape, lambda s, p, n: (0, p[0])),
            pl.BlockSpec(shape, lambda s, p, n: (0, 1 - p[0])),
        ]
        operands += [array, array]
    shape = (weight.shape[0] // 2,) + weight.shape[1:]
    specs += [
        pl.BlockSpec(shape, lambda s, p, n: (p[0], 0, 0)),
        pl.BlockSpec(shape, lambda s, p, n: (1 - p[0], 0, 0)),
    ]
    operands += [weight, weight]
    cross = (16, 256 * (win // 16) + weight.shape[2])
    shapes = [(win, width), (win, width + 384), (win, 256), cross, cross]
    return pl.pallas_call(
        prepare_kernel,
        grid_spec=pltpu.PrefetchScalarGridSpec(
            num_scalar_prefetch=2,
            grid=(1,),
            in_specs=specs,
            out_specs=[pl.BlockSpec(shape, lambda s, p, n: (0, 0)) for shape in shapes],
        ),
        out_shape=[jax.ShapeDtypeStruct(shape, jnp.bfloat16) for shape in shapes],
        compiler_params=pltpu.CompilerParams(vmem_limit_bytes=56 * MIB),
    )(plane, length, *operands)


def attend_kernel(length, q_own, q_peer, *refs, scale, heads, count, first, last):
    refs = list(refs)
    pairs = []
    for _ in range(count):
        block = refs.pop(0)
        span = 256 * max(1, 256 // block.shape[0])
        for start in range(0, block.shape[1], span):
            groups = range(start, start + span, 256)
            pairs.append(
                (
                    jnp.concatenate([block[:, g : g + 128] for g in groups], axis=0),
                    jnp.concatenate([block[:, g + 128 : g + 256] for g in groups], axis=0),
                )
            )
    if first:
        comp, peer_keys, peer_values, peer_length = (refs.pop(0) for _ in range(4))
        pairs.append(
            (
                jnp.concatenate([comp[:, :128], peer_keys[...]], axis=0),
                jnp.concatenate([comp[:, 128:], peer_values[...]], axis=0),
            )
        )
    else:
        acc_in, stats_in = refs.pop(0), refs.pop(0)
    out = refs.pop(0)
    win = q_own.shape[0]
    rows = 2 * win
    if first:
        row = lax.broadcasted_iota(jnp.int32, (rows, rows), 0)
        slot = lax.broadcasted_iota(jnp.int32, (rows, rows), 1)
        far_slot = (slot - win).astype(jnp.float32)
        bound = peer_length[0:1, 0:1].astype(jnp.float32)
        own = (row < win) & (slot <= row) & (slot < length[0])
        peer = (row >= win) & (slot >= win) & (slot <= row) & (far_slot < bound)
        seen = own | peer

    def score(h):
        cols = slice(h * 128, h * 128 + 128)
        q = jnp.concatenate([q_own[:, cols], q_peer[:, cols]], axis=0)
        scores = [
            lax.dot_general(
                q, keys, (((1,), (1,)), ((), ())), preferred_element_type=jnp.float32
            )
            for keys, _ in pairs
        ]
        if first:
            scores[-1] = jnp.where(seen, scores[-1], -jnp.inf)
        return scores

    if not last:
        lane = lax.broadcasted_iota(jnp.int32, (rows, 128), 1)
        found = jnp.zeros((rows, 128), jnp.float32)
    ahead = score(0)
    for h in range(heads):
        cols = slice(h * 128, h * 128 + 128)
        scores = ahead
        if h + 1 < heads:
            ahead = score(h + 1)
        peak = None
        for block in scores:
            for j in range(0, block.shape[1], 128):
                piece = block[:, j : j + 128]
                peak = piece if peak is None else jnp.maximum(peak, piece)
        top = jnp.max(peak, axis=-1, keepdims=True)
        if not first:
            old = stats_in[:, h : h + 1]
            top = jnp.maximum(top, old)
            factor = jnp.exp2((old - top) * scale)
        acc = None
        for block, (_, values) in zip(scores, pairs):
            weights = jnp.exp2((block - top) * scale).astype(jnp.bfloat16)
            wide = jnp.concatenate([values, jnp.ones_like(values)], axis=1)
            part = jnp.dot(weights, wide, preferred_element_type=jnp.float32)
            acc = part if acc is None else acc + part
        summed, total = acc[:, :128], acc[:, 128:]
        if not first:
            summed = summed + acc_in[:, cols] * factor
            total = total + stats_in[:, heads + h : heads + h + 1] * factor
        if last:
            out[:, cols] = (summed / total).astype(jnp.bfloat16)
        else:
            out[:, cols] = summed
            found = jnp.where(lane == h, top, found)
            found = jnp.where(lane == heads + h, total, found)
    if not last:
        refs[0][...] = found


def attend(length, q_own, pair, blocks, scale, comp=None, state=None, last=False):
    heads = HEADS
    win, width = q_own.shape
    rows = 2 * win
    steps = width // (128 * heads)
    columns = width // 128
    operands = list(blocks)
    lanes = 256 * (win // 16)
    specs = [pl.BlockSpec((b.shape[0], lanes), lambda s: (0, 0)) for b in blocks]
    if comp is not None:
        operands += [comp, pair, pair, pair]
        specs.append(pl.BlockSpec(comp.shape, lambda s: (0, 0)))
        for offset in range(3):
            specs.append(pl.BlockSpec((win, 128), lambda s, o=offset: (0, columns + o)))
    else:
        operands += state
        specs += [
            pl.BlockSpec((rows, 128 * heads), lambda s: (0, s)),
            pl.BlockSpec((rows, 128), lambda s: (0, s)),
        ]
    qspec = pl.BlockSpec((win, 128 * heads), lambda s: (0, s))
    keys = sum(b.shape[0] * lanes // 256 for b in blocks)
    out_specs = [pl.BlockSpec((rows, 128 * heads), lambda s: (0, s))]
    out_shape = [jax.ShapeDtypeStruct((rows, width), jnp.bfloat16 if last else jnp.float32)]
    if not last:
        out_specs.append(pl.BlockSpec((rows, 128), lambda s: (0, s)))
        out_shape.append(jax.ShapeDtypeStruct((rows, 128 * steps), jnp.float32))
    return pl.pallas_call(
        functools.partial(
            attend_kernel,
            scale=scale,
            heads=heads,
            count=len(blocks),
            first=comp is not None,
            last=last,
        ),
        grid=(steps,),
        in_specs=[pl.BlockSpec(memory_space=pltpu.SMEM), qspec, qspec] + specs,
        out_specs=out_specs,
        out_shape=out_shape,
        compiler_params=pltpu.CompilerParams(vmem_limit_bytes=30 * MIB),
        cost_estimate=pl.CostEstimate(
            flops=rows * columns * keys * 128 * 8,
            bytes_accessed=4 * 2**20,
            transcendentals=rows * columns * keys,
        ),
    )(length, q_own, pair, *operands)


def project_kernel(place, *refs, count, arrange):
    refs = list(refs)
    ins = [refs.pop(0) for _ in range(1 if arrange else 2)]
    weights = [[refs.pop(0) for _ in range(n)] for n in count]
    outs = [refs.pop(0), refs.pop(0)]
    if arrange:
        (attended,), ins = ins, refs
        features = attended.shape[1]

        @pl.when(pl.program_id(0) == 0)
        def _():
            row = lax.broadcasted_iota(jnp.int32, (256, 1), 0)
            column = lax.broadcasted_iota(jnp.int32, (256, features), 1)
            plane, z, y = place[0], place[1], place[2]
            totals = [None, None]
            for pair in range(features // 256):
                head = 2 * pair + row // 128
                feature = row % 128
                other = (feature // 64) ^ plane
                dz = (feature // 8 % NZ + NZ - z) % NZ
                dy = (feature // 2 % NY + NY - y) % NY
                z_at = jnp.where(dz < NZ // 2, 2 * dz, 2 * NZ - 1 - 2 * dz)
                y_ring = jnp.where(dy < NY // 2, 2 * dy, 2 * NY - 1 - 2 * dy)
                y_sent = (NY - dy) % NY
                within = other * 16 + head * 2 + feature % 2
                targets = (
                    (y_ring * NZ + z_at) * 32 + within,
                    (z_at * NY + y_sent) * 32 + within,
                )
                block = attended[:, 256 * pair : 256 * pair + 256]
                for k, target in enumerate(targets):
                    moved = jnp.where(column == target, 1.0, 0.0).astype(jnp.bfloat16)
                    part = jnp.dot(block, moved, preferred_element_type=jnp.float32)
                    totals[k] = part if totals[k] is None else totals[k] + part
            for total, ref in zip(totals, ins):
                ref[...] = total.astype(jnp.bfloat16)

    for step, out in enumerate(outs):

        @pl.when(pl.program_id(0) == step)
        def _():
            start = 0
            for rows, pieces in zip(ins, weights):
                weight = jnp.concatenate([p[...] for p in pieces], axis=0)
                width = weight.shape[1]
                out[:, start : start + width] = jnp.dot(
                    rows[...], weight, preferred_element_type=jnp.float32
                ).astype(jnp.bfloat16)
                start += width


def project(place, ins, first, second, offset, side):
    arrange = len(ins) == 1
    rows, features = ins[0].shape
    rest = second[0].shape[1] // 4
    block = CUT + rest
    whole = pl.BlockSpec((rows, features), lambda s, at: (0, 0))

    def column(s, at):
        return 2 * (at[4] ^ side) + (at[3] ^ (1 - s))

    specs = [whole] * len(ins)
    for p in first:
        specs.append(
            pl.BlockSpec((p.shape[0], CUT), lambda s, at: (0, offset // CUT + column(s, at)))
        )
    for p in second:
        specs.append(pl.BlockSpec((p.shape[0], rest), lambda s, at: (0, column(s, at))))
    out_specs = [pl.BlockSpec((rows, block), lambda s, at: (0, 0))] * 2
    out_shape = [jax.ShapeDtypeStruct((rows, block), jnp.bfloat16)] * 2
    if arrange:
        out_specs += [whole, whole]
        out_shape += [jax.ShapeDtypeStruct((rows, features), jnp.bfloat16)] * 2
    return pl.pallas_call(
        functools.partial(project_kernel, count=(len(first), len(second)), arrange=arrange),
        grid_spec=pltpu.PrefetchScalarGridSpec(
            num_scalar_prefetch=1, grid=(2,), in_specs=specs, out_specs=out_specs
        ),
        out_shape=out_shape,
        compiler_params=pltpu.CompilerParams(vmem_limit_bytes=20 * MIB),
        cost_estimate=pl.CostEstimate(
            flops=4 * rows * features * block,
            bytes_accessed=6 * 2**20,
            transcendentals=0,
        ),
    )(place, *ins, *first, *second)


def per_device(
    queries, comp_keys, comp_values, prompt_keys, prompt_values, page_table, lengths, out_weight
):
    win = queries.shape[0]
    head_size = 128
    heads = queries.shape[1] // head_size
    page = prompt_keys.shape[0]
    seq_count = XL * NZ * NY
    width = out_weight.shape[2]
    seq_index = lax.axis_index("seq")
    tp_index = lax.axis_index("tp")
    place = jnp.stack(
        [seq_index // (NZ * NY), seq_index // NY % NZ, seq_index % NY, tp_index % 2, tp_index // 2]
    ).astype(jnp.int32)
    slots = jnp.arange(win, dtype=jnp.int32)

    positions = jnp.concatenate(
        [page * seq_count + slots, page_table[0] * page + jnp.arange(page, dtype=jnp.int32)]
    )
    q_own, pair, comp, own, give = prepare(
        place[:1],
        lengths,
        *tables(positions, head_size),
        queries,
        comp_keys,
        comp_values,
        prompt_keys,
        prompt_values,
        out_weight,
    )
    both = jnp.concatenate([own, across(give)], axis=0)

    lanes = 256 * (win // 16)
    cut = lanes + 4 * CUT
    first, second = both[:, :cut], both[:, cut:]
    up = down = first
    pieces = [first]
    for hop in range(1, NZ // 2):
        up, down = along_z(up, 1), along_z(down, -1)
        pieces += [up, down]
        if hop == 1:
            up, down, second, pair = lax.optimization_barrier((up, down, second, pair))
            pair = across(pair)
            second = [second] + [along_y(second, k) for k in range(1, NY)]
    half = first.shape[0] // 2
    second = jnp.concatenate(second, axis=0)
    last = [along_z(up[:half], 1), along_z(down[half:], -1)]
    first, second = lax.optimization_barrier((jnp.concatenate(pieces, axis=0), second))
    z_up, z_down = along_z(second, 1), along_z(second, -1)
    first = jnp.concatenate([first] + last, axis=0)

    first, pair = lax.optimization_barrier((first, pair))
    scale = LOG2E / math.sqrt(head_size)
    run = functools.partial(attend, lengths, q_own, pair, scale=scale)
    half = first.shape[0] // 2
    y_up, y_down = along_y(first, 1), along_y(first, -1)
    state = run([first], comp=comp)
    z_up, z_down, state = lax.optimization_barrier((z_up, z_down, state))
    first, second = [first, y_up, y_down], [second, z_up, z_down]
    first += [along_y(y_up[:half], 1), along_y(y_down[half:], -1)]
    z_up, z_down = along_z(z_up, 1), along_z(z_down, -1)
    z_up, z_down, state = lax.optimization_barrier((z_up, z_down, state))
    second += [z_up, z_down]
    state = run(first[1:3], state=state)
    z_up, z_down = along_z(z_up, 1), along_z(z_down, -1)
    second += [z_up, z_down]
    half = z_up.shape[0] // 2
    second += [along_z(z_up[:half], 1), along_z(z_down[half:], -1)]
    (attended,) = run(first[3:], state=state, last=True)

    def add(keep, give):
        came = lax.ppermute(give, "tp", [(0, 1), (1, 0), (2, 3), (3, 2)])
        return (keep.astype(jnp.float32) + came.astype(jnp.float32)).astype(jnp.bfloat16)

    axes = ("seq", "tp")
    give, keep, *placed = project(place, [attended], first, second, lanes, 1)
    chip = add(keep, give)
    one = lax.ppermute(chip[:win], axes, both_perm(0, 2))
    three = lax.ppermute(chip[win:], axes, both_perm(1, 2))
    give, keep = project(place, placed, first, second, lanes, 0)
    chip = add(keep, give)
    two = lax.ppermute(chip[win:], axes, both_perm(1, 0))
    result = chip[:win].astype(jnp.float32) + two.astype(jnp.float32)
    result = result + one.astype(jnp.float32) + three.astype(jnp.float32)
    return jnp.where((slots < lengths[0])[:, None], result, 0.0).astype(jnp.bfloat16)


def solution(mesh):
    in_specs = (
        P("seq", "tp"),
        P("seq", "tp"),
        P("seq", "tp"),
        P("seq", "tp"),
        P("seq", "tp"),
        P("seq"),
        P("seq"),
        P("tp", "seq", None),
    )
    out_specs = P("seq", "tp")
    return jax.shard_map(
        per_device, mesh=mesh, in_specs=in_specs, out_specs=out_specs, check_vma=False
    )
```

```python
import functools
import math

import jax
import jax.numpy as jnp
from jax import lax
from jax.experimental import pallas as pl
from jax.experimental.pallas import tpu as pltpu
from jax.sharding import PartitionSpec as P

theta_base = 1000000.0
XL, NZ, NY = 2, 8, 4
LOG2E = math.log2(math.e)
MIB = 2**20
HEADS = 4
CUT = 256


def seq_id(x, z, y):
    return ((x % XL) * NZ + z % NZ) * NY + y % NY


def seq_perm(dx, dz, dy):
    return [
        (seq_id(x, z, y), seq_id(x + dx, z + dz, y + dy))
        for x in range(XL)
        for z in range(NZ)
        for y in range(NY)
    ]


def both_perm(dx, dt):
    return [
        (4 * seq_id(x, z, y) + t, 4 * seq_id(x + dx, z, y) + t ^ dt)
        for x in range(XL)
        for z in range(NZ)
        for y in range(NY)
        for t in range(4)
    ]


def along_z(x, k):
    return lax.ppermute(x, "seq", seq_perm(0, k, 0))


def along_y(x, k):
    return lax.ppermute(x, "seq", seq_perm(0, 0, k))


def across(x):
    return lax.ppermute(x, "seq", seq_perm(1, 0, 0))


def tables(positions, size):
    half = size // 2
    freq = jnp.power(
        jnp.float32(theta_base), -2.0 * jnp.arange(half, dtype=jnp.float32) / size
    )
    angle = positions.astype(jnp.float32)[:, None] * freq[None, :]
    return jnp.cos(angle), jnp.sin(angle)


def ring(block, move, count):
    up = down = block
    pieces = [block]
    for _ in range(1, count // 2):
        up, down = move(up, 1), move(down, -1)
        pieces += [up, down]
    half = block.shape[0] // 2
    return pieces + [move(up[:half], 1), move(down[half:], -1)]


def tables_of(cosines, sines, rows):
    cosine, sine = cosines[rows, :], sines[rows, :]
    return (
        jnp.concatenate([cosine, cosine], axis=1),
        jnp.concatenate([-sine, sine], axis=1),
    )


def turn(block, cosine, sine):
    block = block.astype(jnp.float32)
    return (block * cosine + pltpu.roll(block, 64, 1) * sine).astype(jnp.bfloat16)


def pages_kernel(
    plane, length, cosines, sines, pk_own, pk_give, pv_own, pv_give, w_own, w_give,
    own_out, give_out,
):
    win = pk_own.shape[0]
    cosine, sine = tables_of(cosines, sines, slice(win, None))
    for out, keys, values, weight in (
        (give_out, pk_give, pv_give, w_give),
        (own_out, pk_own, pv_own, w_own),
    ):
        count = win // 16
        turned = turn(keys[...], cosine, sine)
        for g in range(count):
            rows = slice(16 * g, 16 * g + 16)
            out[:, 256 * g : 256 * g + 128] = turned[rows]
            out[:, 256 * g + 128 : 256 * g + 256] = values[rows, :]
        rows = jnp.concatenate([weight[h] for h in range(weight.shape[0])], axis=0)
        block = weight.shape[2] // 4
        base = 256 * count
        for t in range(4):
            cols = base + t * CUT
            out[:, cols : cols + CUT] = rows[:, t * block : t * block + CUT]
            cols = base + 4 * CUT + t * (block - CUT)
            out[:, cols : cols + block - CUT] = rows[:, t * block + CUT : (t + 1) * block]


def queries_kernel(
    plane, length, cosines, sines, q_own, q_give, ck_own, ck_give, cv_own, cv_give,
    q_out, pair_out, comp_out,
):
    win, width = q_own.shape
    cosine, sine = tables_of(cosines, sines, slice(0, win))
    comp_out[:, :128] = turn(ck_own[...], cosine, sine)
    comp_out[:, 128:] = cv_own[...]
    for h in range(width // 128):
        cols = slice(h * 128, h * 128 + 128)
        q_out[:, cols] = turn(q_own[:, cols], cosine, sine)
        pair_out[:, cols] = turn(q_give[:, cols], cosine, sine)
    pair_out[:, width : width + 128] = turn(ck_give[...], cosine, sine)
    pair_out[:, width + 128 : width + 256] = cv_give[...]
    pair_out[:, width + 256 :] = jnp.full(
        (win, 128), length[0].astype(jnp.float32), jnp.float32
    ).astype(jnp.bfloat16)


def prepare(kernel, shapes, plane, length, cosines, sines, arrays, weight=None):
    whole = pl.BlockSpec(cosines.shape, lambda s, p, n: (0, 0))
    specs, operands = [whole, whole], [cosines, sines]
    for array in arrays:
        shape = (array.shape[0], array.shape[1] // 2)
        specs += [
            pl.BlockSpec(shape, lambda s, p, n: (0, p[0])),
            pl.BlockSpec(shape, lambda s, p, n: (0, 1 - p[0])),
        ]
        operands += [array, array]
    if weight is not None:
        shape = (weight.shape[0] // 2,) + weight.shape[1:]
        specs += [
            pl.BlockSpec(shape, lambda s, p, n: (p[0], 0, 0)),
            pl.BlockSpec(shape, lambda s, p, n: (1 - p[0], 0, 0)),
        ]
        operands += [weight, weight]
    return pl.pallas_call(
        kernel,
        grid_spec=pltpu.PrefetchScalarGridSpec(
            num_scalar_prefetch=2,
            grid=(1,),
            in_specs=specs,
            out_specs=[pl.BlockSpec(shape, lambda s, p, n: (0, 0)) for shape in shapes],
        ),
        out_shape=[jax.ShapeDtypeStruct(shape, jnp.bfloat16) for shape in shapes],
        compiler_params=pltpu.CompilerParams(vmem_limit_bytes=56 * MIB),
        cost_estimate=pl.CostEstimate(
            flops=2**20, bytes_accessed=3 * 2**20, transcendentals=0
        ),
    )(plane, length, *operands)


def attend_kernel(length, q_own, q_peer, *refs, scale, heads, count, first, last):
    refs = list(refs)
    pairs = []
    for _ in range(count):
        block = refs.pop(0)
        span = 256 * max(1, 256 // block.shape[0])
        for start in range(0, block.shape[1], span):
            groups = range(start, start + span, 256)
            pairs.append(
                (
                    jnp.concatenate([block[:, g : g + 128] for g in groups], axis=0),
                    jnp.concatenate([block[:, g + 128 : g + 256] for g in groups], axis=0),
                )
            )
    if first:
        comp, peer_keys, peer_values, peer_length = (refs.pop(0) for _ in range(4))
        pairs.append(
            (
                jnp.concatenate([comp[:, :128], peer_keys[...]], axis=0),
                jnp.concatenate([comp[:, 128:], peer_values[...]], axis=0),
            )
        )
    else:
        acc_in, stats_in = refs.pop(0), refs.pop(0)
    out = refs.pop(0)
    win = q_own.shape[0]
    rows = 2 * win
    if first:
        row = lax.broadcasted_iota(jnp.int32, (rows, rows), 0)
        slot = lax.broadcasted_iota(jnp.int32, (rows, rows), 1)
        far_slot = (slot - win).astype(jnp.float32)
        bound = peer_length[0:1, 0:1].astype(jnp.float32)
        own = (row < win) & (slot <= row) & (slot < length[0])
        peer = (row >= win) & (slot >= win) & (slot <= row) & (far_slot < bound)
        seen = own | peer

    def score(h):
        cols = slice(h * 128, h * 128 + 128)
        q = jnp.concatenate([q_own[:, cols], q_peer[:, cols]], axis=0)
        scores = [
            lax.dot_general(
                q, keys, (((1,), (1,)), ((), ())), preferred_element_type=jnp.float32
            )
            for keys, _ in pairs
        ]
        if first:
            scores[-1] = jnp.where(seen, scores[-1], -jnp.inf)
        return scores

    if not last:
        lane = lax.broadcasted_iota(jnp.int32, (rows, 128), 1)
        found = jnp.zeros((rows, 128), jnp.float32)
    ahead = score(0)
    for h in range(heads):
        cols = slice(h * 128, h * 128 + 128)
        scores = ahead
        if h + 1 < heads:
            ahead = score(h + 1)
        peak = None
        for block in scores:
            for j in range(0, block.shape[1], 128):
                piece = block[:, j : j + 128]
                peak = piece if peak is None else jnp.maximum(peak, piece)
        top = jnp.max(peak, axis=-1, keepdims=True)
        if not first:
            old = stats_in[:, h : h + 1]
            top = jnp.maximum(top, old)
            factor = jnp.exp2((old - top) * scale)
        acc = None
        for block, (_, values) in zip(scores, pairs):
            weights = jnp.exp2((block - top) * scale).astype(jnp.bfloat16)
            wide = jnp.concatenate([values, jnp.ones_like(values)], axis=1)
            part = jnp.dot(weights, wide, preferred_element_type=jnp.float32)
            acc = part if acc is None else acc + part
        summed, total = acc[:, :128], acc[:, 128:]
        if not first:
            summed = summed + acc_in[:, cols] * factor
            total = total + stats_in[:, heads + h : heads + h + 1] * factor
        if last:
            out[:, cols] = (summed / total).astype(jnp.bfloat16)
        else:
            out[:, cols] = summed
            found = jnp.where(lane == h, top, found)
            found = jnp.where(lane == heads + h, total, found)
    if not last:
        refs[0][...] = found


def attend(length, q_own, pair, blocks, scale, comp=None, state=None, last=False):
    heads = HEADS
    win, width = q_own.shape
    rows = 2 * win
    steps = width // (128 * heads)
    columns = width // 128
    operands = list(blocks)
    lanes = 256 * (win // 16)
    specs = [pl.BlockSpec((b.shape[0], lanes), lambda s: (0, 0)) for b in blocks]
    if comp is not None:
        operands += [comp, pair, pair, pair]
        specs.append(pl.BlockSpec(comp.shape, lambda s: (0, 0)))
        for offset in range(3):
            specs.append(pl.BlockSpec((win, 128), lambda s, o=offset: (0, columns + o)))
    else:
        operands += state
        specs += [
            pl.BlockSpec((rows, 128 * heads), lambda s: (0, s)),
            pl.BlockSpec((rows, 128), lambda s: (0, s)),
        ]
    qspec = pl.BlockSpec((win, 128 * heads), lambda s: (0, s))
    keys = sum(b.shape[0] * lanes // 256 for b in blocks)
    out_specs = [pl.BlockSpec((rows, 128 * heads), lambda s: (0, s))]
    out_shape = [jax.ShapeDtypeStruct((rows, width), jnp.bfloat16 if last else jnp.float32)]
    if not last:
        out_specs.append(pl.BlockSpec((rows, 128), lambda s: (0, s)))
        out_shape.append(jax.ShapeDtypeStruct((rows, 128 * steps), jnp.float32))
    return pl.pallas_call(
        functools.partial(
            attend_kernel,
            scale=scale,
            heads=heads,
            count=len(blocks),
            first=comp is not None,
            last=last,
        ),
        grid=(steps,),
        in_specs=[pl.BlockSpec(memory_space=pltpu.SMEM), qspec, qspec] + specs,
        out_specs=out_specs,
        out_shape=out_shape,
        compiler_params=pltpu.CompilerParams(vmem_limit_bytes=30 * MIB),
        cost_estimate=pl.CostEstimate(
            flops=rows * columns * keys * 128 * 8,
            bytes_accessed=4 * 2**20,
            transcendentals=rows * columns * keys,
        ),
    )(length, q_own, pair, *operands)


def project_kernel(place, *refs, count, arrange):
    refs = list(refs)
    ins = [refs.pop(0) for _ in range(1 if arrange else 2)]
    weights = [[refs.pop(0) for _ in range(n)] for n in count]
    outs = [refs.pop(0), refs.pop(0)]
    if arrange:
        (attended,), ins = ins, refs
        features = attended.shape[1]

        @pl.when(pl.program_id(0) == 0)
        def _():
            row = lax.broadcasted_iota(jnp.int32, (256, 1), 0)
            column = lax.broadcasted_iota(jnp.int32, (256, features), 1)
            plane, z, y = place[0], place[1], place[2]
            totals = [None, None]
            for pair in range(features // 256):
                head = 2 * pair + row // 128
                feature = row % 128
                other = (feature // 64) ^ plane
                dz = (feature // 8 % NZ + NZ - z) % NZ
                dy = (feature // 2 % NY + NY - y) % NY
                z_at = jnp.where(dz < NZ // 2, 2 * dz, 2 * NZ - 1 - 2 * dz)
                y_ring = jnp.where(dy < NY // 2, 2 * dy, 2 * NY - 1 - 2 * dy)
                y_sent = (NY - dy) % NY
                within = other * 16 + head * 2 + feature % 2
                targets = (
                    (y_ring * NZ + z_at) * 32 + within,
                    (z_at * NY + y_sent) * 32 + within,
                )
                block = attended[:, 256 * pair : 256 * pair + 256]
                for k, target in enumerate(targets):
                    moved = jnp.where(column == target, 1.0, 0.0).astype(jnp.bfloat16)
                    part = jnp.dot(block, moved, preferred_element_type=jnp.float32)
                    totals[k] = part if totals[k] is None else totals[k] + part
            for total, ref in zip(totals, ins):
                ref[...] = total.astype(jnp.bfloat16)

    for step, out in enumerate(outs):

        @pl.when(pl.program_id(0) == step)
        def _():
            start = 0
            for rows, pieces in zip(ins, weights):
                weight = jnp.concatenate([p[...] for p in pieces], axis=0)
                width = weight.shape[1]
                out[:, start : start + width] = jnp.dot(
                    rows[...], weight, preferred_element_type=jnp.float32
                ).astype(jnp.bfloat16)
                start += width


def project(place, ins, first, second, offset, side):
    arrange = len(ins) == 1
    rows, features = ins[0].shape
    rest = second[0].shape[1] // 4
    block = CUT + rest
    whole = pl.BlockSpec((rows, features), lambda s, at: (0, 0))

    def column(s, at):
        return 2 * (at[4] ^ side) + (at[3] ^ (1 - s))

    specs = [whole] * len(ins)
    for p in first:
        specs.append(
            pl.BlockSpec((p.shape[0], CUT), lambda s, at: (0, offset // CUT + column(s, at)))
        )
    for p in second:
        specs.append(pl.BlockSpec((p.shape[0], rest), lambda s, at: (0, column(s, at))))
    out_specs = [pl.BlockSpec((rows, block), lambda s, at: (0, 0))] * 2
    out_shape = [jax.ShapeDtypeStruct((rows, block), jnp.bfloat16)] * 2
    if arrange:
        out_specs += [whole, whole]
        out_shape += [jax.ShapeDtypeStruct((rows, features), jnp.bfloat16)] * 2
    return pl.pallas_call(
        functools.partial(project_kernel, count=(len(first), len(second)), arrange=arrange),
        grid_spec=pltpu.PrefetchScalarGridSpec(
            num_scalar_prefetch=1, grid=(2,), in_specs=specs, out_specs=out_specs
        ),
        out_shape=out_shape,
        compiler_params=pltpu.CompilerParams(vmem_limit_bytes=20 * MIB),
        cost_estimate=pl.CostEstimate(
            flops=4 * rows * features * block,
            bytes_accessed=6 * 2**20,
            transcendentals=0,
        ),
    )(place, *ins, *first, *second)


def per_device(
    queries, comp_keys, comp_values, prompt_keys, prompt_values, page_table, lengths, out_weight
):
    win = queries.shape[0]
    head_size = 128
    page = prompt_keys.shape[0]
    seq_count = XL * NZ * NY
    width = out_weight.shape[2]
    seq_index = lax.axis_index("seq")
    tp_index = lax.axis_index("tp")
    place = jnp.stack(
        [seq_index // (NZ * NY), seq_index // NY % NZ, seq_index % NY, tp_index % 2, tp_index // 2]
    ).astype(jnp.int32)
    slots = jnp.arange(win, dtype=jnp.int32)

    positions = jnp.concatenate(
        [page * seq_count + slots, page_table[0] * page + jnp.arange(page, dtype=jnp.int32)]
    )
    shared = (place[:1], lengths, *tables(positions, head_size))
    cross = (16, 256 * (win // 16) + width)
    own, give = prepare(
        pages_kernel, [cross, cross], *shared, [prompt_keys, prompt_values], out_weight
    )
    half = queries.shape[1] // 2
    q_own, pair, comp = prepare(
        queries_kernel,
        [(win, half), (win, half + 384), (win, 256)],
        *shared,
        [queries, comp_keys, comp_values],
    )
    both = jnp.concatenate([own, across(give)], axis=0)

    lanes = 256 * (win // 16)
    cut = lanes + 4 * CUT
    first, second = both[:, :cut], both[:, cut:]
    up = down = first
    pieces = [first]
    for hop in range(1, NZ // 2):
        up, down = along_z(up, 1), along_z(down, -1)
        pieces += [up, down]
        if hop == 1:
            up, down, second, pair = lax.optimization_barrier((up, down, second, pair))
            pair = across(pair)
            second = [second] + [along_y(second, k) for k in range(1, NY)]
    half = first.shape[0] // 2
    second = jnp.concatenate(second, axis=0)
    last = [along_z(up[:half], 1), along_z(down[half:], -1)]
    first, second = lax.optimization_barrier((jnp.concatenate(pieces, axis=0), second))
    z_up, z_down = along_z(second, 1), along_z(second, -1)
    first = jnp.concatenate([first] + last, axis=0)

    first, pair = lax.optimization_barrier((first, pair))
    scale = LOG2E / math.sqrt(head_size)
    run = functools.partial(attend, lengths, q_own, pair, scale=scale)
    half = first.shape[0] // 2
    y_up, y_down = along_y(first, 1), along_y(first, -1)
    state = run([first], comp=comp)
    z_up, z_down, state = lax.optimization_barrier((z_up, z_down, state))
    first, second = [first, y_up, y_down], [second, z_up, z_down]
    first += [along_y(y_up[:half], 1), along_y(y_down[half:], -1)]
    z_up, z_down = along_z(z_up, 1), along_z(z_down, -1)
    z_up, z_down, state = lax.optimization_barrier((z_up, z_down, state))
    second += [z_up, z_down]
    state = run(first[1:3], state=state)
    z_up, z_down = along_z(z_up, 1), along_z(z_down, -1)
    second += [z_up, z_down]
    half = z_up.shape[0] // 2
    second += [along_z(z_up[:half], 1), along_z(z_down[half:], -1)]
    (attended,) = run(first[3:], state=state, last=True)

    def add(keep, give):
        came = lax.ppermute(give, "tp", [(0, 1), (1, 0), (2, 3), (3, 2)])
        return (keep.astype(jnp.float32) + came.astype(jnp.float32)).astype(jnp.bfloat16)

    axes = ("seq", "tp")
    give, keep, *placed = project(place, [attended], first, second, lanes, 1)
    chip = add(keep, give)
    one = lax.ppermute(chip[:win], axes, both_perm(0, 2))
    three = lax.ppermute(chip[win:], axes, both_perm(1, 2))
    give, keep = project(place, placed, first, second, lanes, 0)
    chip = add(keep, give)
    two = lax.ppermute(chip[win:], axes, both_perm(1, 0))
    result = chip[:win].astype(jnp.float32) + two.astype(jnp.float32)
    result = result + one.astype(jnp.float32) + three.astype(jnp.float32)
    return jnp.where((slots < lengths[0])[:, None], result, 0.0).astype(jnp.bfloat16)


def solution(mesh):
    in_specs = (
        P("seq", "tp"),
        P("seq", "tp"),
        P("seq", "tp"),
        P("seq", "tp"),
        P("seq", "tp"),
        P("seq"),
        P("seq"),
        P("tp", "seq", None),
    )
    out_specs = P("seq", "tp")
    return jax.shard_map(
        per_device, mesh=mesh, in_specs=in_specs, out_specs=out_specs, check_vma=False
    )
```

```python
import functools
import math

import jax
import jax.numpy as jnp
from jax import lax
from jax.experimental import pallas as pl
from jax.experimental.pallas import tpu as pltpu
from jax.sharding import PartitionSpec as P

theta_base = 1000000.0
XL, NZ, NY = 2, 8, 4
LOG2E = math.log2(math.e)
MIB = 2**20
HEADS = 4
CUT = 256


def seq_id(x, z, y):
    return ((x % XL) * NZ + z % NZ) * NY + y % NY


def seq_perm(dx, dz, dy):
    return [
        (seq_id(x, z, y), seq_id(x + dx, z + dz, y + dy))
        for x in range(XL)
        for z in range(NZ)
        for y in range(NY)
    ]


def both_perm(dx, dt):
    return [
        (4 * seq_id(x, z, y) + t, 4 * seq_id(x + dx, z, y) + t ^ dt)
        for x in range(XL)
        for z in range(NZ)
        for y in range(NY)
        for t in range(4)
    ]


def along_z(x, k):
    return lax.ppermute(x, "seq", seq_perm(0, k, 0))


def along_y(x, k):
    return lax.ppermute(x, "seq", seq_perm(0, 0, k))


def across(x):
    return lax.ppermute(x, "seq", seq_perm(1, 0, 0))


def tables(positions, size):
    half = size // 2
    freq = jnp.power(
        jnp.float32(theta_base), -2.0 * jnp.arange(half, dtype=jnp.float32) / size
    )
    angle = positions.astype(jnp.float32)[:, None] * freq[None, :]
    return jnp.cos(angle), jnp.sin(angle)


def ring(block, move, count):
    up = down = block
    pieces = [block]
    for _ in range(1, count // 2):
        up, down = move(up, 1), move(down, -1)
        pieces += [up, down]
    half = block.shape[0] // 2
    return pieces + [move(up[:half], 1), move(down[half:], -1)]


def tables_of(cosines, sines, rows):
    cosine, sine = cosines[rows, :], sines[rows, :]
    return (
        jnp.concatenate([cosine, cosine], axis=1),
        jnp.concatenate([-sine, sine], axis=1),
    )


def turn(block, cosine, sine):
    block = block.astype(jnp.float32)
    return (block * cosine + pltpu.roll(block, 64, 1) * sine).astype(jnp.bfloat16)


def pages_kernel(
    plane, length, cosines, sines, pk_own, pk_give, pv_own, pv_give, w_own, w_give,
    own_out, give_out,
):
    win = pk_own.shape[0]
    cosine, sine = tables_of(cosines, sines, slice(win, None))
    for out, keys, values, weight in (
        (give_out, pk_give, pv_give, w_give),
        (own_out, pk_own, pv_own, w_own),
    ):
        count = win // 16
        turned = turn(keys[...], cosine, sine)
        for g in range(count):
            rows = slice(16 * g, 16 * g + 16)
            out[:, 256 * g : 256 * g + 128] = turned[rows]
            out[:, 256 * g + 128 : 256 * g + 256] = values[rows, :]
        rows = jnp.concatenate([weight[h] for h in range(weight.shape[0])], axis=0)
        block = weight.shape[2] // 4
        base = 256 * count
        for t in range(4):
            cols = base + t * CUT
            out[:, cols : cols + CUT] = rows[:, t * block : t * block + CUT]
            cols = base + 4 * CUT + t * (block - CUT)
            out[:, cols : cols + block - CUT] = rows[:, t * block + CUT : (t + 1) * block]


def queries_kernel(
    plane, length, cosines, sines, q_own, q_give, ck_own, ck_give, cv_own, cv_give,
    q_out, pair_out, comp_out,
):
    win, width = q_own.shape
    cosine, sine = tables_of(cosines, sines, slice(0, win))
    comp_out[:, :128] = turn(ck_own[...], cosine, sine)
    comp_out[:, 128:] = cv_own[...]
    for h in range(width // 128):
        cols = slice(h * 128, h * 128 + 128)
        q_out[:, cols] = turn(q_own[:, cols], cosine, sine)
        pair_out[:, cols] = turn(q_give[:, cols], cosine, sine)
    pair_out[:, width : width + 128] = turn(ck_give[...], cosine, sine)
    pair_out[:, width + 128 : width + 256] = cv_give[...]
    pair_out[:, width + 256 :] = jnp.full(
        (win, 128), length[0].astype(jnp.float32), jnp.float32
    ).astype(jnp.bfloat16)


def prepare(kernel, shapes, plane, length, cosines, sines, arrays, weight=None):
    whole = pl.BlockSpec(cosines.shape, lambda s, p, n: (0, 0))
    specs, operands = [whole, whole], [cosines, sines]
    for array in arrays:
        shape = (array.shape[0], array.shape[1] // 2)
        specs += [
            pl.BlockSpec(shape, lambda s, p, n: (0, p[0])),
            pl.BlockSpec(shape, lambda s, p, n: (0, 1 - p[0])),
        ]
        operands += [array, array]
    if weight is not None:
        shape = (weight.shape[0] // 2,) + weight.shape[1:]
        specs += [
            pl.BlockSpec(shape, lambda s, p, n: (p[0], 0, 0)),
            pl.BlockSpec(shape, lambda s, p, n: (1 - p[0], 0, 0)),
        ]
        operands += [weight, weight]
    return pl.pallas_call(
        kernel,
        grid_spec=pltpu.PrefetchScalarGridSpec(
            num_scalar_prefetch=2,
            grid=(1,),
            in_specs=specs,
            out_specs=[pl.BlockSpec(shape, lambda s, p, n: (0, 0)) for shape in shapes],
        ),
        out_shape=[jax.ShapeDtypeStruct(shape, jnp.bfloat16) for shape in shapes],
        compiler_params=pltpu.CompilerParams(vmem_limit_bytes=56 * MIB),
        cost_estimate=pl.CostEstimate(
            flops=2**20, bytes_accessed=3 * 2**20, transcendentals=0
        ),
    )(plane, length, *operands)


def attend_kernel(length, q_own, q_peer, *refs, scale, heads, count, first, last):
    refs = list(refs)
    pairs = []
    for _ in range(count):
        block = refs.pop(0)
        span = 256 * max(1, 256 // block.shape[0])
        for start in range(0, block.shape[1], span):
            groups = range(start, start + span, 256)
            pairs.append(
                (
                    jnp.concatenate([block[:, g : g + 128] for g in groups], axis=0),
                    jnp.concatenate([block[:, g + 128 : g + 256] for g in groups], axis=0),
                )
            )
    if first:
        comp, peer_keys, peer_values, peer_length = (refs.pop(0) for _ in range(4))
        pairs.append(
            (
                jnp.concatenate([comp[:, :128], peer_keys[...]], axis=0),
                jnp.concatenate([comp[:, 128:], peer_values[...]], axis=0),
            )
        )
    else:
        acc_in, stats_in = refs.pop(0), refs.pop(0)
    out = refs.pop(0)
    win = q_own.shape[0]
    rows = 2 * win
    if first:
        row = lax.broadcasted_iota(jnp.int32, (rows, rows), 0)
        slot = lax.broadcasted_iota(jnp.int32, (rows, rows), 1)
        far_slot = (slot - win).astype(jnp.float32)
        bound = peer_length[0:1, 0:1].astype(jnp.float32)
        own = (row < win) & (slot <= row) & (slot < length[0])
        peer = (row >= win) & (slot >= win) & (slot <= row) & (far_slot < bound)
        seen = own | peer

    def score(h):
        cols = slice(h * 128, h * 128 + 128)
        q = jnp.concatenate([q_own[:, cols], q_peer[:, cols]], axis=0)
        scores = [
            lax.dot_general(
                q, keys, (((1,), (1,)), ((), ())), preferred_element_type=jnp.float32
            )
            for keys, _ in pairs
        ]
        if first:
            scores[-1] = jnp.where(seen, scores[-1], -jnp.inf)
        return scores

    if not last:
        lane = lax.broadcasted_iota(jnp.int32, (rows, 128), 1)
        found = jnp.zeros((rows, 128), jnp.float32)
    ahead = score(0)
    for h in range(heads):
        cols = slice(h * 128, h * 128 + 128)
        scores = ahead
        if h + 1 < heads:
            ahead = score(h + 1)
        peak = None
        for block in scores:
            for j in range(0, block.shape[1], 128):
                piece = block[:, j : j + 128]
                peak = piece if peak is None else jnp.maximum(peak, piece)
        top = jnp.max(peak, axis=-1, keepdims=True)
        if not first:
            old = stats_in[:, h : h + 1]
            top = jnp.maximum(top, old)
            factor = jnp.exp2((old - top) * scale)
        acc = None
        for block, (_, values) in zip(scores, pairs):
            weights = jnp.exp2((block - top) * scale).astype(jnp.bfloat16)
            wide = jnp.concatenate([values, jnp.ones_like(values)], axis=1)
            part = jnp.dot(weights, wide, preferred_element_type=jnp.float32)
            acc = part if acc is None else acc + part
        summed, total = acc[:, :128], acc[:, 128:]
        if not first:
            summed = summed + acc_in[:, cols] * factor
            total = total + stats_in[:, heads + h : heads + h + 1] * factor
        if last:
            out[:, cols] = (summed / total).astype(jnp.bfloat16)
        else:
            out[:, cols] = summed
            found = jnp.where(lane == h, top, found)
            found = jnp.where(lane == heads + h, total, found)
    if not last:
        refs[0][...] = found


def attend(length, q_own, pair, blocks, scale, comp=None, state=None, last=False):
    heads = HEADS
    win, width = q_own.shape
    rows = 2 * win
    steps = width // (128 * heads)
    columns = width // 128
    operands = list(blocks)
    lanes = 256 * (win // 16)
    specs = [pl.BlockSpec((b.shape[0], lanes), lambda s: (0, 0)) for b in blocks]
    if comp is not None:
        operands += [comp, pair, pair, pair]
        specs.append(pl.BlockSpec(comp.shape, lambda s: (0, 0)))
        for offset in range(3):
            specs.append(pl.BlockSpec((win, 128), lambda s, o=offset: (0, columns + o)))
    else:
        operands += state
        specs += [
            pl.BlockSpec((rows, 128 * heads), lambda s: (0, s)),
            pl.BlockSpec((rows, 128), lambda s: (0, s)),
        ]
    qspec = pl.BlockSpec((win, 128 * heads), lambda s: (0, s))
    keys = sum(b.shape[0] * lanes // 256 for b in blocks)
    out_specs = [pl.BlockSpec((rows, 128 * heads), lambda s: (0, s))]
    out_shape = [jax.ShapeDtypeStruct((rows, width), jnp.bfloat16 if last else jnp.float32)]
    if not last:
        out_specs.append(pl.BlockSpec((rows, 128), lambda s: (0, s)))
        out_shape.append(jax.ShapeDtypeStruct((rows, 128 * steps), jnp.float32))
    return pl.pallas_call(
        functools.partial(
            attend_kernel,
            scale=scale,
            heads=heads,
            count=len(blocks),
            first=comp is not None,
            last=last,
        ),
        grid=(steps,),
        in_specs=[pl.BlockSpec(memory_space=pltpu.SMEM), qspec, qspec] + specs,
        out_specs=out_specs,
        out_shape=out_shape,
        compiler_params=pltpu.CompilerParams(vmem_limit_bytes=24 * MIB),
        cost_estimate=pl.CostEstimate(
            flops=rows * columns * keys * 128 * 8,
            bytes_accessed=4 * 2**20,
            transcendentals=rows * columns * keys,
        ),
    )(length, q_own, pair, *operands)


def project_kernel(place, *refs, count, arrange):
    refs = list(refs)
    ins = [refs.pop(0) for _ in range(1 if arrange else 2)]
    weights = [[refs.pop(0) for _ in range(n)] for n in count]
    outs = [refs.pop(0), refs.pop(0)]
    if arrange:
        (attended,), ins = ins, refs
        features = attended.shape[1]

        @pl.when(pl.program_id(0) == 0)
        def _():
            row = lax.broadcasted_iota(jnp.int32, (256, 1), 0)
            column = lax.broadcasted_iota(jnp.int32, (256, features), 1)
            plane, z, y = place[0], place[1], place[2]
            totals = [None, None]
            for pair in range(features // 256):
                head = 2 * pair + row // 128
                feature = row % 128
                other = (feature // 64) ^ plane
                dz = (feature // 8 % NZ + NZ - z) % NZ
                dy = (feature // 2 % NY + NY - y) % NY
                z_at = jnp.where(dz < NZ // 2, 2 * dz, 2 * NZ - 1 - 2 * dz)
                y_ring = jnp.where(dy < NY // 2, 2 * dy, 2 * NY - 1 - 2 * dy)
                y_sent = (NY - dy) % NY
                within = other * 16 + head * 2 + feature % 2
                targets = (
                    (y_ring * NZ + z_at) * 32 + within,
                    (z_at * NY + y_sent) * 32 + within,
                )
                block = attended[:, 256 * pair : 256 * pair + 256]
                for k, target in enumerate(targets):
                    moved = jnp.where(column == target, 1.0, 0.0).astype(jnp.bfloat16)
                    part = jnp.dot(block, moved, preferred_element_type=jnp.float32)
                    totals[k] = part if totals[k] is None else totals[k] + part
            for total, ref in zip(totals, ins):
                ref[...] = total.astype(jnp.bfloat16)

    for step, out in enumerate(outs):

        @pl.when(pl.program_id(0) == step)
        def _():
            start = 0
            for rows, pieces in zip(ins, weights):
                weight = jnp.concatenate([p[...] for p in pieces], axis=0)
                width = weight.shape[1]
                out[:, start : start + width] = jnp.dot(
                    rows[...], weight, preferred_element_type=jnp.float32
                ).astype(jnp.bfloat16)
                start += width


def project(place, ins, first, second, offset, side):
    arrange = len(ins) == 1
    rows, features = ins[0].shape
    rest = second[0].shape[1] // 4
    block = CUT + rest
    whole = pl.BlockSpec((rows, features), lambda s, at: (0, 0))

    def column(s, at):
        return 2 * (at[4] ^ side) + (at[3] ^ (1 - s))

    specs = [whole] * len(ins)
    for p in first:
        specs.append(
            pl.BlockSpec((p.shape[0], CUT), lambda s, at: (0, offset // CUT + column(s, at)))
        )
    for p in second:
        specs.append(pl.BlockSpec((p.shape[0], rest), lambda s, at: (0, column(s, at))))
    out_specs = [pl.BlockSpec((rows, block), lambda s, at: (0, 0))] * 2
    out_shape = [jax.ShapeDtypeStruct((rows, block), jnp.bfloat16)] * 2
    if arrange:
        out_specs += [whole, whole]
        out_shape += [jax.ShapeDtypeStruct((rows, features), jnp.bfloat16)] * 2
    return pl.pallas_call(
        functools.partial(project_kernel, count=(len(first), len(second)), arrange=arrange),
        grid_spec=pltpu.PrefetchScalarGridSpec(
            num_scalar_prefetch=1, grid=(2,), in_specs=specs, out_specs=out_specs
        ),
        out_shape=out_shape,
        compiler_params=pltpu.CompilerParams(vmem_limit_bytes=16 * MIB),
        cost_estimate=pl.CostEstimate(
            flops=4 * rows * features * block,
            bytes_accessed=6 * 2**20,
            transcendentals=0,
        ),
    )(place, *ins, *first, *second)


def per_device(
    queries, comp_keys, comp_values, prompt_keys, prompt_values, page_table, lengths, out_weight
):
    win = queries.shape[0]
    head_size = 128
    page = prompt_keys.shape[0]
    seq_count = XL * NZ * NY
    width = out_weight.shape[2]
    seq_index = lax.axis_index("seq")
    tp_index = lax.axis_index("tp")
    place = jnp.stack(
        [seq_index // (NZ * NY), seq_index // NY % NZ, seq_index % NY, tp_index % 2, tp_index // 2]
    ).astype(jnp.int32)
    slots = jnp.arange(win, dtype=jnp.int32)

    positions = jnp.concatenate(
        [page * seq_count + slots, page_table[0] * page + jnp.arange(page, dtype=jnp.int32)]
    )
    shared = (place[:1], lengths, *tables(positions, head_size))
    cross = (16, 256 * (win // 16) + width)
    own, give = prepare(
        pages_kernel, [cross, cross], *shared, [prompt_keys, prompt_values], out_weight
    )
    half = queries.shape[1] // 2
    q_own, pair, comp = prepare(
        queries_kernel,
        [(win, half), (win, half + 384), (win, 256)],
        *shared,
        [queries, comp_keys, comp_values],
    )
    both = jnp.concatenate([own, across(give)], axis=0)

    lanes = 256 * (win // 16)
    cut = lanes + 4 * CUT
    first, second = both[:, :cut], both[:, cut:]
    up = down = first
    pieces = [first]
    for hop in range(1, NZ // 2):
        up, down = along_z(up, 1), along_z(down, -1)
        pieces += [up, down]
        if hop == 1:
            up, down, second, pair = lax.optimization_barrier((up, down, second, pair))
            pair = across(pair)
            second = [second] + [along_y(second, k) for k in range(1, NY)]
    half = first.shape[0] // 2
    second = jnp.concatenate(second, axis=0)
    last = [along_z(up[:half], 1), along_z(down[half:], -1)]
    first, second = lax.optimization_barrier((jnp.concatenate(pieces, axis=0), second))
    z_up, z_down = along_z(second, 1), along_z(second, -1)
    first = jnp.concatenate([first] + last, axis=0)

    first, pair = lax.optimization_barrier((first, pair))
    scale = LOG2E / math.sqrt(head_size)
    run = functools.partial(attend, lengths, q_own, pair, scale=scale)
    half = first.shape[0] // 2
    y_up, y_down = along_y(first, 1), along_y(first, -1)
    state = run([first], comp=comp)
    z_up, z_down, state = lax.optimization_barrier((z_up, z_down, state))
    first, second = [first, y_up, y_down], [second, z_up, z_down]
    first += [along_y(y_up[:half], 1), along_y(y_down[half:], -1)]
    z_up, z_down = along_z(z_up, 1), along_z(z_down, -1)
    z_up, z_down, state = lax.optimization_barrier((z_up, z_down, state))
    second += [z_up, z_down]
    state = run(first[1:3], state=state)
    z_up, z_down = along_z(z_up, 1), along_z(z_down, -1)
    second += [z_up, z_down]
    half = z_up.shape[0] // 2
    second += [along_z(z_up[:half], 1), along_z(z_down[half:], -1)]
    (attended,) = run(first[3:], state=state, last=True)

    def add(keep, give):
        came = lax.ppermute(give, "tp", [(0, 1), (1, 0), (2, 3), (3, 2)])
        return (keep.astype(jnp.float32) + came.astype(jnp.float32)).astype(jnp.bfloat16)

    axes = ("seq", "tp")
    give, keep, *placed = project(place, [attended], first, second, lanes, 1)
    chip = add(keep, give)
    one = lax.ppermute(chip[:win], axes, both_perm(0, 2))
    three = lax.ppermute(chip[win:], axes, both_perm(1, 2))
    give, keep = project(place, placed, first, second, lanes, 0)
    chip = add(keep, give)
    two = lax.ppermute(chip[win:], axes, both_perm(1, 0))
    result = chip[:win].astype(jnp.float32) + two.astype(jnp.float32)
    result = result + one.astype(jnp.float32) + three.astype(jnp.float32)
    return jnp.where((slots < lengths[0])[:, None], result, 0.0).astype(jnp.bfloat16)


def solution(mesh):
    in_specs = (
        P("seq", "tp"),
        P("seq", "tp"),
        P("seq", "tp"),
        P("seq", "tp"),
        P("seq", "tp"),
        P("seq"),
        P("seq"),
        P("tp", "seq", None),
    )
    out_specs = P("seq", "tp")
    return jax.shard_map(
        per_device, mesh=mesh, in_specs=in_specs, out_specs=out_specs, check_vma=False
    )
```

```python
import functools
import math

import jax
import jax.numpy as jnp
from jax import lax
from jax.experimental import pallas as pl
from jax.experimental.pallas import tpu as pltpu
from jax.sharding import PartitionSpec as P

theta_base = 1000000.0
XL, NZ, NY = 2, 8, 4
LOG2E = math.log2(math.e)
MIB = 2**20
HEADS = 8
CUT = 256


def seq_id(x, z, y):
    return ((x % XL) * NZ + z % NZ) * NY + y % NY


def seq_perm(dx, dz, dy):
    return [
        (seq_id(x, z, y), seq_id(x + dx, z + dz, y + dy))
        for x in range(XL)
        for z in range(NZ)
        for y in range(NY)
    ]


def both_perm(dx, dt):
    return [
        (4 * seq_id(x, z, y) + t, 4 * seq_id(x + dx, z, y) + t ^ dt)
        for x in range(XL)
        for z in range(NZ)
        for y in range(NY)
        for t in range(4)
    ]


def along_z(x, k):
    return lax.ppermute(x, "seq", seq_perm(0, k, 0))


def along_y(x, k):
    return lax.ppermute(x, "seq", seq_perm(0, 0, k))


def across(x):
    return lax.ppermute(x, "seq", seq_perm(1, 0, 0))


def tables(positions, size):
    half = size // 2
    freq = jnp.power(
        jnp.float32(theta_base), -2.0 * jnp.arange(half, dtype=jnp.float32) / size
    )
    angle = positions.astype(jnp.float32)[:, None] * freq[None, :]
    return jnp.cos(angle), jnp.sin(angle)


def ring(block, move, count):
    up = down = block
    pieces = [block]
    for _ in range(1, count // 2):
        up, down = move(up, 1), move(down, -1)
        pieces += [up, down]
    half = block.shape[0] // 2
    return pieces + [move(up[:half], 1), move(down[half:], -1)]


def tables_of(cosines, sines, rows):
    cosine, sine = cosines[rows, :], sines[rows, :]
    return (
        jnp.concatenate([cosine, cosine], axis=1),
        jnp.concatenate([-sine, sine], axis=1),
    )


def turn(block, cosine, sine):
    block = block.astype(jnp.float32)
    return (block * cosine + pltpu.roll(block, 64, 1) * sine).astype(jnp.bfloat16)


def pages_kernel(
    plane, length, cosines, sines, pk_own, pk_give, pv_own, pv_give, w_own, w_give,
    own_out, give_out,
):
    win = pk_own.shape[0]
    cosine, sine = tables_of(cosines, sines, slice(win, None))
    for out, keys, values, weight in (
        (give_out, pk_give, pv_give, w_give),
        (own_out, pk_own, pv_own, w_own),
    ):
        count = win // 16
        turned = turn(keys[...], cosine, sine)
        for g in range(count):
            rows = slice(16 * g, 16 * g + 16)
            out[:, 256 * g : 256 * g + 128] = turned[rows]
            out[:, 256 * g + 128 : 256 * g + 256] = values[rows, :]
        rows = jnp.concatenate([weight[h] for h in range(weight.shape[0])], axis=0)
        block = weight.shape[2] // 4
        base = 256 * count
        for t in range(4):
            cols = base + t * CUT
            out[:, cols : cols + CUT] = rows[:, t * block : t * block + CUT]
            cols = base + 4 * CUT + t * (block - CUT)
            out[:, cols : cols + block - CUT] = rows[:, t * block + CUT : (t + 1) * block]


def queries_kernel(
    plane, length, cosines, sines, q_own, q_give, ck_own, ck_give, cv_own, cv_give,
    q_out, pair_out, comp_out,
):
    win, width = q_own.shape
    cosine, sine = tables_of(cosines, sines, slice(0, win))
    comp_out[:, :128] = turn(ck_own[...], cosine, sine)
    comp_out[:, 128:] = cv_own[...]
    for h in range(width // 128):
        cols = slice(h * 128, h * 128 + 128)
        q_out[:, cols] = turn(q_own[:, cols], cosine, sine)
        pair_out[:, cols] = turn(q_give[:, cols], cosine, sine)
    pair_out[:, width : width + 128] = turn(ck_give[...], cosine, sine)
    pair_out[:, width + 128 : width + 256] = cv_give[...]
    pair_out[:, width + 256 :] = jnp.full(
        (win, 128), length[0].astype(jnp.float32), jnp.float32
    ).astype(jnp.bfloat16)


def prepare(kernel, shapes, plane, length, cosines, sines, arrays, weight=None):
    whole = pl.BlockSpec(cosines.shape, lambda s, p, n: (0, 0))
    specs, operands = [whole, whole], [cosines, sines]
    for array in arrays:
        shape = (array.shape[0], array.shape[1] // 2)
        specs += [
            pl.BlockSpec(shape, lambda s, p, n: (0, p[0])),
            pl.BlockSpec(shape, lambda s, p, n: (0, 1 - p[0])),
        ]
        operands += [array, array]
    if weight is not None:
        shape = (weight.shape[0] // 2,) + weight.shape[1:]
        specs += [
            pl.BlockSpec(shape, lambda s, p, n: (p[0], 0, 0)),
            pl.BlockSpec(shape, lambda s, p, n: (1 - p[0], 0, 0)),
        ]
        operands += [weight, weight]
    return pl.pallas_call(
        kernel,
        grid_spec=pltpu.PrefetchScalarGridSpec(
            num_scalar_prefetch=2,
            grid=(1,),
            in_specs=specs,
            out_specs=[pl.BlockSpec(shape, lambda s, p, n: (0, 0)) for shape in shapes],
        ),
        out_shape=[jax.ShapeDtypeStruct(shape, jnp.bfloat16) for shape in shapes],
        compiler_params=pltpu.CompilerParams(vmem_limit_bytes=56 * MIB),
        cost_estimate=pl.CostEstimate(
            flops=2**20, bytes_accessed=3 * 2**20, transcendentals=0
        ),
    )(plane, length, *operands)


def attend_kernel(length, q_own, q_peer, *refs, scale, heads, count, first, last):
    refs = list(refs)
    pairs = []
    for _ in range(count):
        block = refs.pop(0)
        span = 256 * max(1, 256 // block.shape[0])
        for start in range(0, block.shape[1], span):
            groups = range(start, start + span, 256)
            pairs.append(
                (
                    jnp.concatenate([block[:, g : g + 128] for g in groups], axis=0),
                    jnp.concatenate([block[:, g + 128 : g + 256] for g in groups], axis=0),
                )
            )
    if first:
        comp, peer_keys, peer_values, peer_length = (refs.pop(0) for _ in range(4))
        pairs.append(
            (
                jnp.concatenate([comp[:, :128], peer_keys[...]], axis=0),
                jnp.concatenate([comp[:, 128:], peer_values[...]], axis=0),
            )
        )
    else:
        acc_in, stats_in = refs.pop(0), refs.pop(0)
    out = refs.pop(0)
    win = q_own.shape[0]
    rows = 2 * win
    if first:
        row = lax.broadcasted_iota(jnp.int32, (rows, rows), 0)
        slot = lax.broadcasted_iota(jnp.int32, (rows, rows), 1)
        far_slot = (slot - win).astype(jnp.float32)
        bound = peer_length[0:1, 0:1].astype(jnp.float32)
        own = (row < win) & (slot <= row) & (slot < length[0])
        peer = (row >= win) & (slot >= win) & (slot <= row) & (far_slot < bound)
        seen = own | peer

    def score(h):
        cols = slice(h * 128, h * 128 + 128)
        q = jnp.concatenate([q_own[:, cols], q_peer[:, cols]], axis=0)
        scores = [
            lax.dot_general(
                q, keys, (((1,), (1,)), ((), ())), preferred_element_type=jnp.float32
            )
            for keys, _ in pairs
        ]
        if first:
            scores[-1] = jnp.where(seen, scores[-1], -jnp.inf)
        return scores

    if not last:
        lane = lax.broadcasted_iota(jnp.int32, (rows, 128), 1)
        found = jnp.zeros((rows, 128), jnp.float32)
    ahead = score(0)
    for h in range(heads):
        cols = slice(h * 128, h * 128 + 128)
        scores = ahead
        if h + 1 < heads:
            ahead = score(h + 1)
        peak = None
        for block in scores:
            for j in range(0, block.shape[1], 128):
                piece = block[:, j : j + 128]
                peak = piece if peak is None else jnp.maximum(peak, piece)
        top = jnp.max(peak, axis=-1, keepdims=True)
        if not first:
            old = stats_in[:, h : h + 1]
            top = jnp.maximum(top, old)
            factor = jnp.exp2((old - top) * scale)
        acc = None
        for block, (_, values) in zip(scores, pairs):
            weights = jnp.exp2((block - top) * scale).astype(jnp.bfloat16)
            wide = jnp.concatenate([values, jnp.ones_like(values)], axis=1)
            part = jnp.dot(weights, wide, preferred_element_type=jnp.float32)
            acc = part if acc is None else acc + part
        summed, total = acc[:, :128], acc[:, 128:]
        if not first:
            summed = summed + acc_in[:, cols] * factor
            total = total + stats_in[:, heads + h : heads + h + 1] * factor
        if last:
            out[:, cols] = (summed / total).astype(jnp.bfloat16)
        else:
            out[:, cols] = summed
            found = jnp.where(lane == h, top, found)
            found = jnp.where(lane == heads + h, total, found)
    if not last:
        refs[0][...] = found


def attend(length, q_own, pair, blocks, scale, comp=None, state=None, last=False):
    heads = HEADS
    win, width = q_own.shape
    rows = 2 * win
    steps = width // (128 * heads)
    columns = width // 128
    operands = list(blocks)
    lanes = 256 * (win // 16)
    specs = [pl.BlockSpec((b.shape[0], lanes), lambda s: (0, 0)) for b in blocks]
    if comp is not None:
        operands += [comp, pair, pair, pair]
        specs.append(pl.BlockSpec(comp.shape, lambda s: (0, 0)))
        for offset in range(3):
            specs.append(pl.BlockSpec((win, 128), lambda s, o=offset: (0, columns + o)))
    else:
        operands += state
        specs += [
            pl.BlockSpec((rows, 128 * heads), lambda s: (0, s)),
            pl.BlockSpec((rows, 128), lambda s: (0, s)),
        ]
    qspec = pl.BlockSpec((win, 128 * heads), lambda s: (0, s))
    keys = sum(b.shape[0] * lanes // 256 for b in blocks)
    out_specs = [pl.BlockSpec((rows, 128 * heads), lambda s: (0, s))]
    out_shape = [jax.ShapeDtypeStruct((rows, width), jnp.bfloat16 if last else jnp.float32)]
    if not last:
        out_specs.append(pl.BlockSpec((rows, 128), lambda s: (0, s)))
        out_shape.append(jax.ShapeDtypeStruct((rows, 128 * steps), jnp.float32))
    return pl.pallas_call(
        functools.partial(
            attend_kernel,
            scale=scale,
            heads=heads,
            count=len(blocks),
            first=comp is not None,
            last=last,
        ),
        grid=(steps,),
        in_specs=[pl.BlockSpec(memory_space=pltpu.SMEM), qspec, qspec] + specs,
        out_specs=out_specs,
        out_shape=out_shape,
        compiler_params=pltpu.CompilerParams(vmem_limit_bytes=30 * MIB),
        cost_estimate=pl.CostEstimate(
            flops=rows * columns * keys * 128 * 8,
            bytes_accessed=4 * 2**20,
            transcendentals=rows * columns * keys,
        ),
    )(length, q_own, pair, *operands)


def project_kernel(place, *refs, count, arrange):
    refs = list(refs)
    ins = [refs.pop(0) for _ in range(1 if arrange else 2)]
    weights = [[refs.pop(0) for _ in range(n)] for n in count]
    outs = [refs.pop(0), refs.pop(0)]
    if arrange:
        (attended,), ins = ins, refs
        features = attended.shape[1]

        @pl.when(pl.program_id(0) == 0)
        def _():
            row = lax.broadcasted_iota(jnp.int32, (256, 1), 0)
            column = lax.broadcasted_iota(jnp.int32, (256, features), 1)
            plane, z, y = place[0], place[1], place[2]
            totals = [None, None]
            for pair in range(features // 256):
                head = 2 * pair + row // 128
                feature = row % 128
                other = (feature // 64) ^ plane
                dz = (feature // 8 % NZ + NZ - z) % NZ
                dy = (feature // 2 % NY + NY - y) % NY
                z_at = jnp.where(dz < NZ // 2, 2 * dz, 2 * NZ - 1 - 2 * dz)
                y_ring = jnp.where(dy < NY // 2, 2 * dy, 2 * NY - 1 - 2 * dy)
                y_sent = (NY - dy) % NY
                within = other * 16 + head * 2 + feature % 2
                targets = (
                    (y_ring * NZ + z_at) * 32 + within,
                    (z_at * NY + y_sent) * 32 + within,
                )
                block = attended[:, 256 * pair : 256 * pair + 256]
                for k, target in enumerate(targets):
                    moved = jnp.where(column == target, 1.0, 0.0).astype(jnp.bfloat16)
                    part = jnp.dot(block, moved, preferred_element_type=jnp.float32)
                    totals[k] = part if totals[k] is None else totals[k] + part
            for total, ref in zip(totals, ins):
                ref[...] = total.astype(jnp.bfloat16)

    for step, out in enumerate(outs):

        @pl.when(pl.program_id(0) == step)
        def _():
            start = 0
            for rows, pieces in zip(ins, weights):
                weight = jnp.concatenate([p[...] for p in pieces], axis=0)
                width = weight.shape[1]
                out[:, start : start + width] = jnp.dot(
                    rows[...], weight, preferred_element_type=jnp.float32
                ).astype(jnp.bfloat16)
                start += width


def project(place, ins, first, second, offset, side):
    arrange = len(ins) == 1
    rows, features = ins[0].shape
    rest = second[0].shape[1] // 4
    block = CUT + rest
    whole = pl.BlockSpec((rows, features), lambda s, at: (0, 0))

    def column(s, at):
        return 2 * (at[4] ^ side) + (at[3] ^ (1 - s))

    specs = [whole] * len(ins)
    for p in first:
        specs.append(
            pl.BlockSpec((p.shape[0], CUT), lambda s, at: (0, offset // CUT + column(s, at)))
        )
    for p in second:
        specs.append(pl.BlockSpec((p.shape[0], rest), lambda s, at: (0, column(s, at))))
    out_specs = [pl.BlockSpec((rows, block), lambda s, at: (0, 0))] * 2
    out_shape = [jax.ShapeDtypeStruct((rows, block), jnp.bfloat16)] * 2
    if arrange:
        out_specs += [whole, whole]
        out_shape += [jax.ShapeDtypeStruct((rows, features), jnp.bfloat16)] * 2
    return pl.pallas_call(
        functools.partial(project_kernel, count=(len(first), len(second)), arrange=arrange),
        grid_spec=pltpu.PrefetchScalarGridSpec(
            num_scalar_prefetch=1, grid=(2,), in_specs=specs, out_specs=out_specs
        ),
        out_shape=out_shape,
        compiler_params=pltpu.CompilerParams(vmem_limit_bytes=20 * MIB),
        cost_estimate=pl.CostEstimate(
            flops=4 * rows * features * block,
            bytes_accessed=6 * 2**20,
            transcendentals=0,
        ),
    )(place, *ins, *first, *second)


def per_device(
    queries, comp_keys, comp_values, prompt_keys, prompt_values, page_table, lengths, out_weight
):
    win = queries.shape[0]
    head_size = 128
    page = prompt_keys.shape[0]
    seq_count = XL * NZ * NY
    width = out_weight.shape[2]
    seq_index = lax.axis_index("seq")
    tp_index = lax.axis_index("tp")
    place = jnp.stack(
        [seq_index // (NZ * NY), seq_index // NY % NZ, seq_index % NY, tp_index % 2, tp_index // 2]
    ).astype(jnp.int32)
    slots = jnp.arange(win, dtype=jnp.int32)

    positions = jnp.concatenate(
        [page * seq_count + slots, page_table[0] * page + jnp.arange(page, dtype=jnp.int32)]
    )
    shared = (place[:1], lengths, *tables(positions, head_size))
    cross = (16, 256 * (win // 16) + width)
    own, give = prepare(
        pages_kernel, [cross, cross], *shared, [prompt_keys, prompt_values], out_weight
    )
    half = queries.shape[1] // 2
    q_own, pair, comp = prepare(
        queries_kernel,
        [(win, half), (win, half + 384), (win, 256)],
        *shared,
        [queries, comp_keys, comp_values],
    )
    both = jnp.concatenate([own, across(give)], axis=0)

    lanes = 256 * (win // 16)
    cut = lanes + 4 * CUT
    first, second = both[:, :cut], both[:, cut:]
    up = down = first
    pieces = [first]
    for hop in range(1, NZ // 2):
        up, down = along_z(up, 1), along_z(down, -1)
        pieces += [up, down]
        if hop == 1:
            up, down, second, pair = lax.optimization_barrier((up, down, second, pair))
            pair = across(pair)
            second = [second] + [along_y(second, k) for k in range(1, NY)]
    half = first.shape[0] // 2
    second = jnp.concatenate(second, axis=0)
    last = [along_z(up[:half], 1), along_z(down[half:], -1)]
    first, second = lax.optimization_barrier((jnp.concatenate(pieces, axis=0), second))
    z_up, z_down = along_z(second, 1), along_z(second, -1)
    first = jnp.concatenate([first] + last, axis=0)

    first, pair = lax.optimization_barrier((first, pair))
    scale = LOG2E / math.sqrt(head_size)
    run = functools.partial(attend, lengths, q_own, pair, scale=scale)
    half = first.shape[0] // 2
    y_up, y_down = along_y(first, 1), along_y(first, -1)
    state = run([first], comp=comp)
    z_up, z_down, state = lax.optimization_barrier((z_up, z_down, state))
    first, second = [first, y_up, y_down], [second, z_up, z_down]
    first += [along_y(y_up[:half], 1), along_y(y_down[half:], -1)]
    z_up, z_down = along_z(z_up, 1), along_z(z_down, -1)
    z_up, z_down, state = lax.optimization_barrier((z_up, z_down, state))
    second += [z_up, z_down]
    state = run(first[1:3], state=state)
    z_up, z_down = along_z(z_up, 1), along_z(z_down, -1)
    second += [z_up, z_down]
    half = z_up.shape[0] // 2
    second += [along_z(z_up[:half], 1), along_z(z_down[half:], -1)]
    (attended,) = run(first[3:], state=state, last=True)

    def add(keep, give):
        came = lax.ppermute(give, "tp", [(0, 1), (1, 0), (2, 3), (3, 2)])
        return (keep.astype(jnp.float32) + came.astype(jnp.float32)).astype(jnp.bfloat16)

    axes = ("seq", "tp")
    give, keep, *placed = project(place, [attended], first, second, lanes, 1)
    chip = add(keep, give)
    one = lax.ppermute(chip[:win], axes, both_perm(0, 2))
    three = lax.ppermute(chip[win:], axes, both_perm(1, 2))
    give, keep = project(place, placed, first, second, lanes, 0)
    chip = add(keep, give)
    two = lax.ppermute(chip[win:], axes, both_perm(1, 0))
    result = chip[:win].astype(jnp.float32) + two.astype(jnp.float32)
    result = result + one.astype(jnp.float32) + three.astype(jnp.float32)
    return jnp.where((slots < lengths[0])[:, None], result, 0.0).astype(jnp.bfloat16)


def solution(mesh):
    in_specs = (
        P("seq", "tp"),
        P("seq", "tp"),
        P("seq", "tp"),
        P("seq", "tp"),
        P("seq", "tp"),
        P("seq"),
        P("seq"),
        P("tp", "seq", None),
    )
    out_specs = P("seq", "tp")
    return jax.shard_map(
        per_device, mesh=mesh, in_specs=in_specs, out_specs=out_specs, check_vma=False
    )
```
